512 devices in a mesh: rows: 128 (over x, z, core), cells: 4 (over y).
Axes of the slice: x: 4, y: 4, z: 16, core: 2. Of those that a mesh axis runs over, the one named last changes fastest.
Arguments:
- row_profile: bfloat16 [4, 2097152], P(None, ('rows', 'cells')), may hold values from 0.029907227 to 0.29882812
- col_profile: bfloat16 [16, 2097152], P(None, ('rows', 'cells')), may hold values from 0.029907227 to 0.29882812
- send_list: int32 [262144, 16], P(('rows', 'cells')), may hold values from 0 to 4096, as said below
- tile_list: int32 [16384, 256], P(('rows', 'cells')), may hold values from 0 to 8192, as said below
- row_offset: int32 [16384, 256], P(('rows', 'cells')), may hold values from 0 to 4
- col_offset: int32 [16384, 256], P(('rows', 'cells')), may hold values from 0 to 112
- macro_mask: int32 [4096, 4096], P(('rows', 'cells')), may hold values 0 or 1
Outputs:
- fields: bfloat16 [2, 4096, 4096], P(None, ('rows', 'cells'))
- force: float32 [2, 2097152], P(None, ('rows', 'cells'))
The draws below stay inside these ranges and needn't reach their ends.
Inputs may be any that keep to these rules, and one draw needn't show every extreme that they name: `send_list`: in row s * 512 + d the filled slots come first and hold distinct cells of block s; every cell of a block is listed exactly once over its 512 rows; 4096 marks an empty slot; every cell block fills all 16 slots of some rows. `tile_list`: each bin block receives exactly 4096 filled slots, and each of them is listed exactly once over that block's 32 tiles; filled places come first in a row; 8192 marks an empty place; every bin block has tiles with all 256 places filled.
All inputs are finite; a program needn't handle non-finite values. No bound on the sum of `macro_mask` on one device may be relied on, other than what follows from the above.
Results may differ from the reference program's by a relative error of at most 0.0017.
Values may be sent and summed in bfloat16 or wider, within the bound.
No kernel may reach another device: no remote copies, remote signals or barrier semaphores. Data moves between devices by JAX's collectives and lax.ppermute only.
A program may use at most 64 MiB of HBM per device.

```python
import jax
import jax.numpy as jnp
from jax import lax

G = 4096
TW = 128
BH = 4
BW = 16
CELL_DEV = 4096
NCELL = 2097152
TH = 8
NT = 32
CAP = 16
TCAP = 256
N_ROWS = 128
N_CELLS = 4
DEVICES = 512


def level_pattern(key, how_many, mean_count):
    key_first, key_second, key_order = jax.random.split(key, 3)
    quarter = how_many // 4
    first_part = jax.random.randint(key_first, (quarter,), 0, mean_count + 1, dtype=jnp.int32)
    second_part = jax.random.randint(key_second, (quarter,), 0, mean_count + 1, dtype=jnp.int32)
    values = jnp.concatenate([jnp.full((quarter,), 2 * mean_count, jnp.int32), first_part, second_part, 2 * mean_count - first_part - second_part])
    return jax.random.permutation(key_order, values)


def routing(key):
    per_pair = CELL_DEV // DEVICES
    per_tile = CELL_DEV // NT
    key_list = jax.random.split(key, 6)
    pattern = level_pattern(key_list[0], DEVICES, per_pair)
    sigma = jax.random.permutation(key_list[1], DEVICES)
    shifts = jax.random.permutation(key_list[2], DEVICES)
    counts = pattern[(shifts[:, None] + sigma[None, :]) % DEVICES]
    orders = jax.vmap(lambda sub_key: jax.random.permutation(sub_key, CELL_DEV))(jax.random.split(key_list[3], DEVICES)).astype(jnp.int32)
    starts = jnp.cumsum(counts, axis=1) - counts
    slot_index = jnp.arange(CAP, dtype=jnp.int32)
    where_at = jnp.minimum(starts[:, :, None] + slot_index, CELL_DEV - 1).reshape(DEVICES, DEVICES * CAP)
    listed = jnp.take_along_axis(orders, where_at, axis=1).reshape(DEVICES, DEVICES, CAP)
    send_table = jnp.where(slot_index < counts[:, :, None], listed, CELL_DEV).reshape(DEVICES * DEVICES, CAP).astype(jnp.int32)
    filled = (slot_index[None, None, :] < counts.T[:, :, None]).reshape(DEVICES, DEVICES * CAP)
    ranks = jax.vmap(lambda sub_key: jax.random.permutation(sub_key, DEVICES * CAP))(jax.random.split(key_list[4], DEVICES)).astype(jnp.int32)
    scores = jnp.where(filled, ranks, DEVICES * CAP + ranks)
    arrival = jnp.argsort(scores, axis=1).astype(jnp.int32)
    tile_counts = jax.vmap(lambda sub_key: level_pattern(sub_key, NT, per_tile))(jax.random.split(key_list[5], DEVICES))
    tile_starts = jnp.cumsum(tile_counts, axis=1) - tile_counts
    place_index = jnp.arange(TCAP, dtype=jnp.int32)
    tile_at = jnp.minimum(tile_starts[:, :, None] + place_index, CELL_DEV - 1).reshape(DEVICES, NT * TCAP)
    tile_listed = jnp.take_along_axis(arrival, tile_at, axis=1).reshape(DEVICES, NT, TCAP)
    tile_table = jnp.where(place_index < tile_counts[:, :, None], tile_listed, DEVICES * CAP).reshape(DEVICES * NT, TCAP).astype(jnp.int32)
    return (send_table, tile_table)


def draw_send_list(key, part):
    return routing(key)[0]


def draw_tile_list(key, part):
    return routing(key)[1]


def set_ends(values, own_key, smallest, largest):
    dims = values.shape
    index_at = [jax.random.randint(jax.random.fold_in(own_key, axis), (), 0, dims[axis]) for axis in range(len(dims))]
    values = values.at[tuple(index_at)].set(smallest)
    longest = dims.index(max(dims))
    index_at[longest] = (index_at[longest] + 1) % dims[longest]
    return values.at[tuple(index_at)].set(largest)


def level_of(rng, shape, shards, low, top_value):
    factor_of = 1.0
    for axis_at, parts in shards:
        draws = jax.random.uniform(jax.random.fold_in(jax.random.fold_in(rng, 6), axis_at), (parts,), jnp.float32, low / len(shards), top_value / len(shards))
        factor_of = factor_of * jnp.repeat(jnp.exp(draws), shape[axis_at] // parts).reshape((-1,) + (1,) * (len(shape) - 1 - axis_at))
    return factor_of


def setup_inputs(seed: int = 0) -> dict:
    key_of = jax.random.split(jax.random.key(seed), 8)
    row_profile = jnp.clip(0.029907227 + 0.2689209 * jax.random.uniform(key_of[0], (BH, NCELL), jnp.float32) ** level_of(key_of[0], (BH, NCELL), ((1, 512),), -0.2, 0.2), 0.029907227, 0.29882812).astype(jnp.bfloat16)
    col_profile = jnp.clip(0.029907227 + 0.2689209 * jax.random.uniform(key_of[1], (BW, NCELL), jnp.float32) ** level_of(key_of[1], (BW, NCELL), ((1, 512),), -0.2, 0.2), 0.029907227, 0.29882812).astype(jnp.bfloat16)
    send_list = draw_send_list(jax.random.fold_in(key_of[7], 71), 0)
    tile_list = draw_tile_list(jax.random.fold_in(key_of[7], 71), 0)
    row_offset = set_ends(jax.random.randint(key_of[4], (DEVICES * NT, TCAP), 0, TH - BH + 1), jax.random.fold_in(key_of[4], 1), 0, TH - BH).astype(jnp.int32)
    col_offset = set_ends(jax.random.randint(key_of[5], (DEVICES * NT, TCAP), 0, TW - BW + 1), jax.random.fold_in(key_of[5], 1), 0, TW - BW).astype(jnp.int32)
    macro_mask = set_ends((jax.random.randint(key_of[6], (G, G), 0, 4) < 1).astype(jnp.int32), jax.random.fold_in(key_of[6], 1), 0, 1)
    return dict(row_profile=row_profile, col_profile=col_profile, send_list=send_list, tile_list=tile_list, row_offset=row_offset, col_offset=col_offset, macro_mask=macro_mask)


MACRO_LEVEL = 4.0


def coefficient(wave_u, wave_v, grid_size):
    freq_u = wave_u * (jnp.pi / grid_size)
    freq_v = wave_v * (jnp.pi / grid_size)
    radius = freq_u * freq_u + freq_v * freq_v
    weight_u = jnp.where(wave_u == 0, 1.0 / grid_size, 2.0 / grid_size)
    weight_v = jnp.where(wave_v == 0, 1.0 / grid_size, 2.0 / grid_size)
    return jnp.where(radius > 0, weight_u * weight_v / jnp.where(radius > 0, radius, 1.0), 0.0)


def cosine_forward(values, axis):
    extent = values.shape[axis]
    spectrum_full = jnp.fft.fft(values, n=2 * extent, axis=axis)
    spectrum_full = lax.slice_in_dim(spectrum_full, 0, extent, axis=axis)
    view_shape = [1, 1]
    view_shape[axis] = extent
    angle_steps = (jnp.arange(extent, dtype=jnp.float32) * (jnp.pi / (2.0 * extent))).reshape(view_shape)
    return jnp.real(spectrum_full) * jnp.cos(angle_steps) + jnp.imag(spectrum_full) * jnp.sin(angle_steps)


def cosine_backward(values, axis):
    extent = values.shape[axis]
    view_shape = [1, 1]
    view_shape[axis] = extent
    angle_steps = (jnp.arange(extent, dtype=jnp.float32) * (jnp.pi / (2.0 * extent))).reshape(view_shape)
    twisted = values * jnp.exp(1j * angle_steps)
    padded_out = jnp.fft.ifft(twisted, n=2 * extent, axis=axis) * (2 * extent)
    kept = lax.slice_in_dim(padded_out, 0, extent, axis=axis)
    return jnp.real(kept), jnp.imag(kept)


def placed(profile_e, offset, extent):
    relative = lax.broadcasted_iota(jnp.int32, (1, extent, 1), 1) - offset[:, None, :]
    inside = (relative >= 0) & (relative < profile_e.shape[0])
    moved = jnp.transpose(profile_e, (1, 0, 2))
    picked = jnp.take_along_axis(moved, jnp.clip(relative, 0, profile_e.shape[0] - 1), axis=1)
    return jnp.where(inside, picked, 0.0)


def reference(row_profile, col_profile, send_list, tile_list, row_offset, col_offset, macro_mask):
    devices = N_ROWS * N_CELLS

    def receiver_cells(receiver):
        places = lax.dynamic_slice_in_dim(tile_list, receiver * NT, NT, 0)
        source = jnp.minimum(places // CAP, devices - 1).astype(jnp.int32)
        within = (places % CAP).astype(jnp.int32)
        rows_of = source * devices + receiver
        local_cell = send_list[rows_of, within]
        is_valid = (places < devices * CAP) & (local_cell < CELL_DEV)
        return jnp.where(is_valid, source * CELL_DEV + local_cell, devices * CELL_DEV).astype(jnp.int32)

    def entry_blocks(receiver):
        cell_ids = receiver_cells(receiver)
        rows_e = jnp.take(row_profile, cell_ids, axis=1, mode="fill", fill_value=0).astype(jnp.float32)
        cols_e = jnp.take(col_profile, cell_ids, axis=1, mode="fill", fill_value=0).astype(jnp.float32)
        rows_shift = lax.dynamic_slice_in_dim(row_offset, receiver * NT, NT, 0)
        cols_shift = lax.dynamic_slice_in_dim(col_offset, receiver * NT, NT, 0)
        return cell_ids, placed(rows_e, rows_shift, TH), placed(cols_e, cols_shift, TW)

    def band_density(receiver):
        cell_ids, tall_block, wide_block = entry_blocks(receiver)
        return jnp.einsum("trk,tjk->rtj", tall_block, wide_block).reshape(TH, NT * TW)

    receivers = jnp.arange(devices, dtype=jnp.int32)
    band_stack = lax.map(band_density, receivers)
    density = band_stack.reshape(G, G) + MACRO_LEVEL * macro_mask.astype(jnp.float32)
    spectrum = cosine_forward(cosine_forward(density, 1), 0)
    wave_u = jnp.arange(G, dtype=jnp.float32).reshape(G, 1)
    wave_v = jnp.arange(G, dtype=jnp.float32).reshape(1, G)
    scaled = spectrum * coefficient(wave_u, wave_v, G)
    freq_u = wave_u * (jnp.pi / G)
    freq_v = wave_v * (jnp.pi / G)
    x_half = cosine_backward(scaled * freq_v, 0)[0]
    field_x = cosine_backward(x_half, 1)[1]
    y_half = cosine_backward(scaled * freq_u, 0)[1]
    field_y = cosine_backward(y_half, 1)[0]
    fields = jnp.stack([field_x, field_y]).astype(jnp.bfloat16)

    def band_force(receiver):
        cell_ids, tall_block, wide_block = entry_blocks(receiver)
        field_band = lax.dynamic_slice_in_dim(fields, receiver * TH, TH, 1).astype(jnp.float32).reshape(2, TH, NT, TW)
        crossed = jnp.einsum("frtj,tjk->ftrk", field_band, wide_block)
        return jnp.sum(crossed * tall_block[None], axis=2) / (BH * BW), cell_ids

    force_entries, cell_stack = lax.map(band_force, receivers)
    values = jnp.moveaxis(force_entries, 1, 0).reshape(2, -1)
    force = jnp.zeros((2, NCELL), jnp.float32).at[:, cell_stack.reshape(-1)].add(values, mode="drop")
    return fields, force
```

```python
import functools
import math

import jax
import jax.numpy as jnp
import numpy as np
from jax import lax
from jax.experimental import pallas as pl
from jax.experimental.pallas import tpu as pltpu
from jax.sharding import Mesh
from jax.sharding import PartitionSpec as P

GRID = 4096
BH = 4
BW = 16
TW = 128
TH = 8
NT = 32
TCAP = 256
CAP = 16
CELL_DEV = 4096
LOW = 256
MACRO_LEVEL = 4.0
SCALE = 8192.0
F32 = jnp.float32
BF16 = jnp.bfloat16
I32 = jnp.int32


def split_host(values):
    top = values.astype(jnp.bfloat16)
    rest = (values - top.astype(np.float64)).astype(jnp.bfloat16)
    return top, rest


@functools.cache
def tables_x():
    q = np.arange(512) // 128
    r = (np.arange(512) % 128) // 16
    f = 16 * q + np.arange(512) % 16
    t = np.arange(256) // 8
    r_in = np.arange(256) % 8
    same = r_in[:, None] == r[None, :]
    turn = np.pi * ((t[:, None] * f[None, :]) % 64) / 32.0
    first = np.concatenate([np.cos(turn) * same, -np.sin(turn) * same], axis=1)
    b = np.arange(128)
    angle = np.pi * (f[None, :] * (2 * b[:, None] + 1)) / 8192.0
    w = np.arange(64)
    wave = np.pi * ((w[:, None] * (2 * b[None, :] + 1)) % 256) / 128.0
    second = np.concatenate([np.cos(wave), np.sin(wave)], axis=1)
    return (
        split_host(first),
        np.cos(angle).astype(np.float32),
        np.sin(angle).astype(np.float32),
        split_host(second),
    )


@functools.cache
def tables_y():
    lane = np.arange(128)
    r, c, l = lane // 16, (lane // 8) % 2, lane % 8
    f = np.arange(128)
    a = np.arange(64)
    turn = np.pi * ((f[:, None] * a[None, :]) % 128) / 64.0
    first = np.concatenate([np.cos(turn), -np.sin(turn)], axis=0)
    h = np.arange(4)
    b = 32 * c[None, :] + 8 * h[:, None] + r[None, :]
    angle = np.pi * (f[None, :, None] * (2 * b[:, None, :] + 1)) / 8192.0
    w = np.arange(256) // 8
    l_out = np.arange(256) % 8
    wave = np.pi * (((2 * b[:, :, None] + 1) * w[None, None, :]) % 128) / 64.0
    same = l[:, None] == l_out[None, :]
    second = np.stack([np.cos(wave) * same[None], np.sin(wave) * same[None]], axis=1)
    return (
        split_host(first),
        np.cos(angle).astype(np.float32),
        np.sin(angle).astype(np.float32),
        split_host(second.reshape(1024, 256)),
    )


def halves(values):
    top = values.astype(BF16)
    return top, (values - top.astype(F32)).astype(BF16)


def dot(left, right):
    return jnp.dot(left, right, preferred_element_type=F32)


def dot_last(left, right):
    return lax.dot_general(left, right, (((1,), (1,)), ((), ())), preferred_element_type=F32)


def dot3(left, right):
    left_top, left_rest = left
    right_top, right_rest = right
    return dot(left_top, right_top) + (dot(left_rest, right_top) + dot(left_top, right_rest))


def one_hot(index_row, extent):
    lines = lax.broadcasted_iota(I32, (extent, index_row.shape[1]), 0)
    return jnp.where(lines == index_row, 1.0, 0.0).astype(BF16)


def join_cores(own, other, core):
    lane_core = (lax.broadcasted_iota(I32, own.shape, 1) // 8) % 2
    moved = jnp.where(core == 0, pltpu.roll(other, 8, 1), pltpu.roll(other, 120, 1))
    return jnp.where(lane_core == core, own, moved)


def pack_kernel(row_ref, col_ref, list_ref, out_ref, low_ref, high_ref, table, cols, rows):
    core = lax.axis_index("c")
    for h in range(16):
        table[h * 16 : h * 16 + 16, :] = col_ref[:, h * LOW : (h + 1) * LOW]
    table[256:320, :] = jnp.concatenate(
        [row_ref[:, h * LOW : (h + 1) * LOW].astype(F32) for h in range(16)], axis=0
    ).astype(BF16)
    listed = list_ref[...].astype(F32).T
    high = jnp.floor(listed * (1.0 / LOW))
    low = listed - high * LOW
    target = lax.broadcasted_iota(I32, (512, 512), 1)
    source = (target % 256) // 4 * 8 + ((target // 256) ^ core) * 4 + target % 4
    move = jnp.where(lax.broadcasted_iota(I32, (512, 512), 0) == source, 1.0, 0.0).astype(BF16)
    high_ref[...] = dot(high.astype(BF16), move).astype(I32)
    low_ref[...] = dot(low.astype(BF16), move).astype(I32)
    upper = lax.broadcasted_iota(I32, (8, 512), 0) // 4

    def pick(k):
        found = dot(table[...], one_hot(low_ref[pl.ds(k, 1), :], LOW))
        place = jnp.broadcast_to(high_ref[pl.ds(k, 1), :], (8, 512))
        col_sum = [jnp.zeros((8, 512), F32) for _ in range(2)]
        for h in range(16):
            here = place == h
            for s in range(2):
                start = h * 16 + s * 8
                col_sum[s] = col_sum[s] + jnp.where(here, found[start : start + 8], 0.0)
        row_sum = jnp.zeros((8, 512), F32)
        for h in range(8):
            start = 256 + h * 8
            row_sum = row_sum + jnp.where(place == 2 * h + upper, found[start : start + 8], 0.0)
        row_sum = row_sum + pltpu.roll(row_sum, 4, 0)
        col_sum = jnp.concatenate(col_sum, axis=0)
        return (col_sum * SCALE).astype(I32), (row_sum * SCALE).astype(I32)

    def step(j, carry):
        row_words = []
        for s in range(2):
            k = 2 * j + s
            col_a, row_a = pick(k)
            col_b, row_b = pick(k + 8)
            cols[pl.ds(pl.multiple_of(k * 16, 16), 16), :] = col_a + (col_b << 16)
            row_words.append(row_a + (row_b << 16))
        rows[pl.ds(pl.multiple_of(j * 8, 8), 8), :] = jnp.where(
            upper == 0, row_words[0], row_words[1]
        )
        return carry

    lax.fori_loop(0, 4, step, 0)
    for c in range(2):
        out_ref[pl.ds(c, 256, stride=3), :] = cols[:, c * 256 : (c + 1) * 256].T
    both = [rows[:, :256], rows[:, 256:]]
    out_ref[pl.ds(2, 256, stride=3), :] = jnp.concatenate(both + both, axis=0).T


def pack_profiles(row_profile, col_profile, send_list):
    return pl.pallas_call(
        pack_kernel,
        out_shape=(
            jax.ShapeDtypeStruct((768, 128), I32),
            jax.ShapeDtypeStruct((16, 512), I32),
            jax.ShapeDtypeStruct((16, 512), I32),
        ),
        scratch_shapes=[
            pltpu.VMEM((320, 256), BF16),
            pltpu.VMEM((128, 512), I32),
            pltpu.VMEM((32, 512), I32),
        ],
        compiler_params=pltpu.CompilerParams(vmem_limit_bytes=32 << 20),
        name="pack_profiles",
    )(row_profile, col_profile, send_list)


def slot_address(slots, core):
    source = slots // 16
    low = source // 8 * 4 + source % 4
    high = (((source // 4) % 2) ^ core) * 16 + slots % 16
    return low, high


def spread_kernel(
    own_ref,
    other_ref,
    list_ref,
    row_ref,
    col_ref,
    mask_ref,
    first_top,
    first_rest,
    turn_cos,
    turn_sin,
    second_top,
    second_rest,
    out_ref,
    wide_ref,
    tall_ref,
    low_ref,
    high_ref,
    table,
    density,
):
    core = lax.axis_index("c")
    for s, ref in enumerate((own_ref, other_ref)):
        words = ref[pl.ds(s, 256, stride=3), :].T
        for part, piece in enumerate((words & 0xFFFF, words >> 16)):
            start = s * 256 + part * 128
            table[start : start + 128, :] = (piece.astype(F32) * (1.0 / SCALE)).astype(BF16)
    own_rows = own_ref[pl.ds(2, 256, stride=3), :].T
    other_rows = other_ref[pl.ds(2, 256, stride=3), :].T
    words = jnp.concatenate([own_rows[:32], other_rows[32:64]], axis=0)
    for part, piece in enumerate((words & 0xFFFF, words >> 16)):
        start = 512 + part * 64
        table[start : start + 64, :] = (piece.astype(F32) * (1.0 / SCALE)).astype(BF16)
    low, high = slot_address(list_ref[...], core)
    low_ref[...] = low
    high_ref[...] = high
    upper = lax.broadcasted_iota(I32, (8, TCAP), 0) // 4

    def step(t, carry):
        found = dot(table[...], one_hot(low_ref[pl.ds(t, 1), :], LOW))
        place = jnp.broadcast_to(high_ref[pl.ds(t, 1), :], (8, TCAP))
        col_sum = [jnp.zeros((8, TCAP), F32) for _ in range(2)]
        for h in range(32):
            here = place == h
            for s in range(2):
                start = h * 16 + s * 8
                col_sum[s] = col_sum[s] + jnp.where(here, found[start : start + 8], 0.0)
        row_sum = jnp.zeros((8, TCAP), F32)
        for part in range(2):
            for s in range(2):
                for j in range(4):
                    start = 512 + part * 64 + s * 32 + j * 8
                    here = place == s * 16 + part * 8 + j * 2 + upper
                    row_sum = row_sum + jnp.where(here, found[start : start + 8], 0.0)
        row_sum = row_sum + pltpu.roll(row_sum, 4, 0)
        tall = jnp.where(upper == 0, row_sum, 0.0)
        row_shift = jnp.broadcast_to(row_ref[pl.ds(t, 1), :], (8, TCAP))
        for shift in (1, 2, 4):
            tall = jnp.where((row_shift & shift) != 0, pltpu.roll(tall, shift, 0), tall)
        col_shift = jnp.broadcast_to(col_ref[pl.ds(t, 1), :], (8, TCAP))
        zero = jnp.zeros((8, TCAP), F32)
        strip = jnp.concatenate(col_sum + [zero], axis=0)
        for shift in (1, 2, 4):
            moves = (col_shift & shift) != 0
            moved = pltpu.roll(strip, shift, 0)
            strip = jnp.concatenate(
                [
                    jnp.where(moves, moved[i * 8 : i * 8 + 8], strip[i * 8 : i * 8 + 8])
                    for i in range(3)
                ],
                axis=0,
            )
        blocks = [strip[i * 8 : i * 8 + 8] for i in range(3)]
        for shift in (1, 2, 4, 8):
            moves = (col_shift & (8 * shift)) != 0
            held = blocks
            blocks = []
            for i in range(min(16, len(held) + shift)):
                stay = held[i] if i < len(held) else zero
                come = held[i - shift] if i >= shift else zero
                blocks.append(jnp.where(moves, come, stay))
        wide = jnp.concatenate(blocks, axis=0).astype(BF16)
        wide_ref[pl.ds(pl.multiple_of(t * 128, 128), 128), :] = wide
        tall_ref[pl.ds(pl.multiple_of(t * 8, 8), 8), :] = tall
        covered = mask_ref[:, pl.ds(pl.multiple_of(t * 128, 128), 128)].astype(F32)
        density[pl.ds(pl.multiple_of(t * 8, 8), 8), :] = (
            dot_last(tall.astype(BF16), wide) + MACRO_LEVEL * covered
        )
        return carry

    lax.fori_loop(0, NT, step, 0)
    turned = halves(density[...].T)
    mixed = dot3(turned, (first_top[...], first_rest[...]))
    real, imag = mixed[:, :512], mixed[:, 512:]
    cos, sin = turn_cos[...], turn_sin[...]
    stacked = jnp.concatenate([real * cos + imag * sin, imag * cos - real * sin], axis=0)
    result = dot3((second_top[...], second_rest[...]), halves(stacked))
    for q in range(4):
        out_ref[q * 64 : q * 64 + 64, :] = result[:, q * 128 : q * 128 + 128]


def spread(own, other, tile_list, row_offset, col_offset, macro_mask):
    first, cos, sin, second = tables_x()
    return pl.pallas_call(
        spread_kernel,
        out_shape=(
            jax.ShapeDtypeStruct((256, 128), F32),
            jax.ShapeDtypeStruct((NT * TW, TCAP), BF16),
            jax.ShapeDtypeStruct((NT * TH, TCAP), F32),
            jax.ShapeDtypeStruct((NT, TCAP), I32),
            jax.ShapeDtypeStruct((NT, TCAP), I32),
        ),
        scratch_shapes=[pltpu.VMEM((640, 256), BF16), pltpu.VMEM((NT * TH, TW), F32)],
        compiler_params=pltpu.CompilerParams(vmem_limit_bytes=40 << 20),
        name="spread",
    )(own, other, tile_list, row_offset, col_offset, macro_mask, *first, cos, sin, *second)


def solve_kernel(
    own_ref,
    other_ref,
    first_top,
    first_rest,
    back_top,
    back_rest,
    turn_cos,
    turn_sin,
    second_top,
    second_rest,
    wave_top,
    wave_rest,
    out_ref,
    held,
):
    core = lax.axis_index("c")
    place = (lax.axis_index("x") * 16 + lax.axis_index("z")) * 4 + lax.axis_index("y")
    held[...] = join_cores(own_ref[...], other_ref[...], core)
    first = (first_top[...], first_rest[...])
    parts = []
    for h in range(4):
        mixed = dot3(first, halves(held[pl.ds(h, 64, stride=4), :]))
        real, imag = mixed[:128], mixed[128:]
        cos, sin = turn_cos[h], turn_sin[h]
        parts += [real * cos + imag * sin, imag * cos - real * sin]
    spectrum = dot3(halves(jnp.concatenate(parts, axis=1)), (second_top[...], second_rest[...]))
    lane = lax.broadcasted_iota(I32, (128, 256), 1)
    wave_u = lax.broadcasted_iota(I32, (128, 256), 0) + 128 * (lane // 8)
    wave_v = (place // 64) * 16 + core * 8 + lane % 8 + 64 * (place % 64)
    freq_u = wave_u.astype(F32) * (math.pi / GRID)
    freq_v = wave_v.astype(F32) * (math.pi / GRID)
    radius = freq_u * freq_u + freq_v * freq_v
    weight_u = jnp.where(wave_u == 0, 1.0 / GRID, 2.0 / GRID)
    weight_v = jnp.where(wave_v == 0, 1.0 / GRID, 2.0 / GRID)
    kernel = jnp.where(
        radius > 0, weight_u * weight_v / jnp.where(radius > 0, radius, 1.0), 0.0
    )
    scaled = spectrum * kernel
    both = jnp.concatenate([scaled * freq_v, scaled * freq_u], axis=0)
    waves = dot3(halves(both), (wave_top[...], wave_rest[...]))
    back = (back_top[...], back_rest[...])
    for h in range(4):
        cos, sin = turn_cos[h], turn_sin[h]
        maps = []
        for m in range(2):
            rows = slice(m * 128, m * 128 + 128)
            real = waves[rows, h * 256 : h * 256 + 128]
            imag = waves[rows, h * 256 + 128 : h * 256 + 256]
            out_real = real * cos - imag * sin
            out_imag = real * sin + imag * cos
            pair = [out_real, out_imag] if m == 0 else [out_imag, -out_real]
            maps.append(jnp.concatenate(pair, axis=0))
        result = dot3(back, halves(jnp.concatenate(maps, axis=1)))
        for m in range(2):
            out_ref[pl.ds(2 * h + m, 64, stride=8), :] = result[:, m * 128 : m * 128 + 128]


def solve_columns(own, other):
    first, cos, sin, second = tables_y()
    back = tuple(np.ascontiguousarray(part.T) for part in first)
    wave = tuple(np.ascontiguousarray(part.T) for part in second)
    return pl.pallas_call(
        solve_kernel,
        out_shape=jax.ShapeDtypeStruct((512, 128), F32),
        scratch_shapes=[pltpu.VMEM((256, 128), F32)],
        compiler_params=pltpu.CompilerParams(vmem_limit_bytes=40 << 20),
        name="solve_columns",
    )(own, other, *first, *back, cos, sin, *second, *wave)


def force_kernel(
    own_ref,
    other_ref,
    wide_ref,
    tall_ref,
    low_ref,
    high_ref,
    wave_top,
    wave_rest,
    turn_cos,
    turn_sin,
    last_top,
    last_rest,
    fields_ref,
    out_ref,
    held,
    field,
    total,
):
    core = lax.axis_index("c")
    held[...] = join_cores(own_ref[...], other_ref[...], core)
    columns = [
        held[pl.ds(q * 128 + m, 64, stride=2), :] for m in range(2) for q in range(4)
    ]
    waves = dot3((wave_top[...], wave_rest[...]), halves(jnp.concatenate(columns, axis=1)))
    cos, sin = turn_cos[...], turn_sin[...]
    maps = []
    for m in range(2):
        real = waves[:128, m * 512 : m * 512 + 512]
        imag = waves[128:, m * 512 : m * 512 + 512]
        out_real = real * cos - imag * sin
        out_imag = real * sin + imag * cos
        pair = [out_imag, -out_real] if m == 0 else [out_real, out_imag]
        maps.append(jnp.concatenate(pair, axis=1))
    result = dot3(halves(jnp.concatenate(maps, axis=0)), (last_top[...], last_rest[...]))
    field[...] = result.T
    total[...] = jnp.zeros_like(total)
    lines = lax.broadcasted_iota(I32, (32, TCAP), 0)

    def step(t, carry):
        here = pl.ds(pl.multiple_of(t * 8, 8), 8)
        tile = field[here, :]
        pair = jnp.concatenate([tile[:, :128], tile[:, 128:]], axis=0).astype(BF16)
        for m in range(2):
            fields_ref[m, :, pl.ds(pl.multiple_of(t * 128, 128), 128)] = pair[
                m * 8 : m * 8 + 8
            ]
        wide = wide_ref[pl.ds(pl.multiple_of(t * 128, 128), 128), :]
        crossed = dot(pair, wide)
        tall = tall_ref[here, :]
        chosen = lines == high_ref[pl.ds(t, 1), :]
        tops, rests = [], []
        for m in range(2):
            force = jnp.sum(crossed[m * 8 : m * 8 + 8] * tall, axis=0, keepdims=True) * (
                1.0 / (BH * BW)
            )
            top = force.astype(BF16).astype(F32)
            tops.append(jnp.where(chosen, top, 0.0))
            rests.append(jnp.where(chosen, force - top, 0.0))
        left = jnp.concatenate(tops + rests, axis=0).astype(BF16)
        total[...] += dot_last(left, one_hot(low_ref[pl.ds(t, 1), :], LOW))
        return carry

    lax.fori_loop(0, NT, step, 0)
    summed = total[:64, :] + total[64:, :]
    out_ref[...] = jnp.concatenate([summed, summed], axis=0).T


def tile_forces(own, other, wide, tall, low, high):
    last, cos, sin, wave = tables_x()
    last = tuple(np.ascontiguousarray(part.T) for part in last)
    wave = tuple(np.ascontiguousarray(part.T) for part in wave)
    return pl.pallas_call(
        force_kernel,
        out_shape=(
            jax.ShapeDtypeStruct((2, TH, GRID), BF16),
            jax.ShapeDtypeStruct((256, 128), F32),
        ),
        scratch_shapes=[
            pltpu.VMEM((512, 128), F32),
            pltpu.VMEM((256, 256), F32),
            pltpu.VMEM((128, 256), F32),
        ],
        compiler_params=pltpu.CompilerParams(vmem_limit_bytes=40 << 20),
        name="tile_forces",
    )(own, other, wide, tall, low, high, *wave, cos, sin, *last)


def gather_kernel(own_ref, other_ref, low_ref, high_ref, out_ref, own, other, total):
    own[...] = own_ref[...].T
    other[...] = other_ref[...].T
    total[...] = jnp.zeros_like(total)
    lines = lax.broadcasted_iota(I32, (16, 512), 0)

    def step(k, carry):
        chosen = lines == high_ref[pl.ds(k, 1), :]
        tops, rests = [], []
        for m in range(2):
            force = jnp.concatenate(
                [own[pl.ds(m * 32 + k, 1), :], other[pl.ds(m * 32 + 16 + k, 1), :]], axis=1
            )
            top = force.astype(BF16).astype(F32)
            tops.append(jnp.where(chosen, top, 0.0))
            rests.append(jnp.where(chosen, force - top, 0.0))
        left = jnp.concatenate(tops + rests, axis=0).astype(BF16)
        total[...] += dot_last(left, one_hot(low_ref[pl.ds(k, 1), :], LOW))
        return carry

    lax.fori_loop(0, CAP, step, 0)
    summed = total[:32, :] + total[32:, :]
    for m in range(2):
        for h in range(16):
            out_ref[m : m + 1, h * LOW : (h + 1) * LOW] = summed[m * 16 + h : m * 16 + h + 1]


def gather_forces(own, other, low, high):
    return pl.pallas_call(
        gather_kernel,
        out_shape=jax.ShapeDtypeStruct((2, CELL_DEV), F32),
        scratch_shapes=[
            pltpu.VMEM((128, 256), F32),
            pltpu.VMEM((128, 256), F32),
            pltpu.VMEM((64, 256), F32),
        ],
        compiler_params=pltpu.CompilerParams(vmem_limit_bytes=32 << 20),
        name="gather_forces",
    )(own, other, low, high)


def exchange(words):
    rows = words.shape[0]
    sent = words.reshape(256, 1, rows // 256 * 128)
    own = lax.all_to_all(sent, ("x", "z", "y"), split_axis=0, concat_axis=0, tiled=True)
    own = own.reshape(rows, 128)
    return own, lax.ppermute(own, "c", [(0, 1), (1, 0)])


def per_device(row_profile, col_profile, send_list, tile_list, row_offset, col_offset, macro_mask):
    words, cell_low, cell_high = pack_profiles(row_profile, col_profile, send_list)
    own, other = exchange(words)
    lines, wide, tall, slot_low, slot_high = spread(
        own, other, tile_list, row_offset, col_offset, macro_mask
    )
    maps = solve_columns(*exchange(lines))
    fields, forces = tile_forces(*exchange(maps), wide, tall, slot_low, slot_high)
    cell_force = gather_forces(*exchange(forces), cell_low, cell_high)
    return (fields, cell_force)


def solution(mesh):
    fine = Mesh(mesh.devices.reshape(4, 16, 2, 4), ("x", "z", "c", "y"))
    every = ("x", "z", "c", "y")
    placed = (P(None, every), P(None, every)) + (P(every, None),) * 5
    return jax.shard_map(
        per_device,
        mesh=fine,
        in_specs=placed,
        out_specs=(P(None, every, None), P(None, every)),
        check_vma=False,
    )
```

```python
import functools
import math

import jax
import jax.numpy as jnp
import numpy as np
from jax import lax
from jax.experimental import pallas as pl
from jax.experimental.pallas import tpu as pltpu
from jax.sharding import Mesh
from jax.sharding import PartitionSpec as P

GRID = 4096
BH = 4
BW = 16
TW = 128
TH = 8
NT = 32
TCAP = 256
CAP = 16
CELL_DEV = 4096
LOW = 256
MACRO_LEVEL = 4.0
SCALE = 8192.0
SPREAD_GROUP = 16
FORCE_GROUP = 16
GATHER_GROUP = 16
F32 = jnp.float32
BF16 = jnp.bfloat16
I32 = jnp.int32


def split_host(values):
    top = values.astype(jnp.bfloat16)
    rest = (values - top.astype(np.float64)).astype(jnp.bfloat16)
    return top, rest


@functools.cache
def tables_x():
    q = np.arange(512) // 128
    r = (np.arange(512) % 128) // 16
    f = 16 * q + np.arange(512) % 16
    t = np.arange(256) // 8
    r_in = np.arange(256) % 8
    same = r_in[:, None] == r[None, :]
    turn = np.pi * ((t[:, None] * f[None, :]) % 64) / 32.0
    first = np.concatenate([np.cos(turn) * same, -np.sin(turn) * same], axis=1)
    b = np.arange(128)
    angle = np.pi * (f[None, :] * (2 * b[:, None] + 1)) / 8192.0
    w = np.arange(64)
    wave = np.pi * ((w[:, None] * (2 * b[None, :] + 1)) % 256) / 128.0
    second = np.concatenate([np.cos(wave), np.sin(wave)], axis=1)
    return (
        split_host(first),
        np.cos(angle).astype(np.float32),
        np.sin(angle).astype(np.float32),
        split_host(second),
    )


@functools.cache
def tables_y():
    lane = np.arange(128)
    r, c, l = lane // 16, (lane // 8) % 2, lane % 8
    f = np.arange(128)
    a = np.arange(64)
    turn = np.pi * ((f[:, None] * a[None, :]) % 128) / 64.0
    first = np.concatenate([np.cos(turn), -np.sin(turn)], axis=0)
    h = np.arange(4)
    b = 32 * c[None, :] + 8 * h[:, None] + r[None, :]
    angle = np.pi * (f[None, :, None] * (2 * b[:, None, :] + 1)) / 8192.0
    w = np.arange(256) // 8
    l_out = np.arange(256) % 8
    wave = np.pi * (((2 * b[:, :, None] + 1) * w[None, None, :]) % 128) / 64.0
    same = l[:, None] == l_out[None, :]
    second = np.stack([np.cos(wave) * same[None], np.sin(wave) * same[None]], axis=1)
    return (
        split_host(first),
        np.cos(angle).astype(np.float32),
        np.sin(angle).astype(np.float32),
        split_host(second.reshape(1024, 256)),
    )


def halves(values):
    top = values.astype(BF16)
    return top, (values - top.astype(F32)).astype(BF16)


def dot(left, right):
    return jnp.dot(left, right, preferred_element_type=F32)


def dot_last(left, right):
    return lax.dot_general(left, right, (((1,), (1,)), ((), ())), preferred_element_type=F32)


def dot3(left, right):
    left_top, left_rest = left
    right_top, right_rest = right
    return dot(left_top, right_top) + (dot(left_rest, right_top) + dot(left_top, right_rest))


def one_hot(index_row, extent):
    shape = (extent, index_row.shape[1])
    lines = lax.broadcasted_iota(I32, shape, 0).astype(BF16)
    index = jnp.broadcast_to(index_row.astype(BF16), shape)
    return jnp.where(lines == index, jnp.ones(shape, BF16), jnp.zeros(shape, BF16))


def choose(blocks, index):
    bit = 1
    while len(blocks) > 1:
        odd = (index & bit) != 0
        blocks = [
            jnp.where(odd, blocks[2 * i + 1], blocks[2 * i]) for i in range(len(blocks) // 2)
        ]
        bit *= 2
    return blocks[0]


def load_all(pairs, sems):
    copies = [
        pltpu.make_async_copy(source, target, sems.at[i])
        for i, (source, target) in enumerate(pairs)
    ]
    for copy in copies:
        copy.start()
    return copies


def join_cores(own, other, core):
    lane_core = (lax.broadcasted_iota(I32, own.shape, 1) // 8) % 2
    moved = jnp.where(core == 0, pltpu.roll(other, 8, 1), pltpu.roll(other, 120, 1))
    return jnp.where(lane_core == core, own, moved)


def pack_kernel(
    row_hbm, col_hbm, list_ref, out_ref, low_ref, high_ref, row_ref, col_ref, table, cols, rows, sems
):
    core = lax.axis_index("c")
    copies = load_all([(col_hbm, col_ref), (row_hbm, row_ref)], sems)
    listed = list_ref[...].astype(F32)
    empty = listed >= CELL_DEV
    high = jnp.floor(listed * (1.0 / LOW))
    low = jnp.where(empty, float(LOW), listed - high * LOW)
    target = lax.broadcasted_iota(I32, (512, 512), 1)
    source = (target % 256) // 4 * 8 + ((target // 256) ^ core) * 4 + target % 4
    move = jnp.where(lax.broadcasted_iota(I32, (512, 512), 0) == source, 1.0, 0.0).astype(BF16)
    high_ref[...] = dot(high.astype(BF16), move).astype(I32)
    low_ref[...] = dot(low.astype(BF16), move).astype(I32)
    for copy in copies:
        copy.wait()
    for h in range(16):
        table[h * 16 : h * 16 + 16, :] = col_ref[:, h * LOW : (h + 1) * LOW]
    table[256:320, :] = jnp.concatenate(
        [row_ref[:, h * LOW : (h + 1) * LOW].astype(F32) for h in range(16)], axis=0
    ).astype(BF16)
    upper = lax.broadcasted_iota(I32, (8, 512), 0) // 4

    def pick(k):
        found = dot(table[...], one_hot(low_ref[pl.ds(k, 1), :], LOW))
        place = jnp.broadcast_to(high_ref[pl.ds(k, 1), :], (8, 512))
        col_sum = jnp.concatenate(
            [
                choose([found[h * 16 + s * 8 : h * 16 + s * 8 + 8] for h in range(16)], place)
                for s in range(2)
            ],
            axis=0,
        )
        row_sum = choose([found[256 + h * 8 : 264 + h * 8] for h in range(8)], place // 2)
        row_sum = jnp.where(place % 2 == upper, row_sum, pltpu.roll(row_sum, 4, 0))
        return (col_sum * SCALE).astype(I32), (row_sum * SCALE).astype(I32)

    def step(j, carry):
        row_words = []
        for s in range(2):
            k = 2 * j + s
            col_a, row_a = pick(k)
            col_b, row_b = pick(k + 8)
            cols[pl.ds(pl.multiple_of(k * 16, 16), 16), :] = col_a + (col_b << 16)
            row_words.append(row_a + (row_b << 16))
        rows[pl.ds(pl.multiple_of(j * 8, 8), 8), :] = jnp.where(
            upper == 0, row_words[0], pltpu.roll(row_words[1], 4, 0)
        )
        return carry

    lax.fori_loop(0, 4, step, 0, unroll=True)
    for c in range(2):
        out_ref[pl.ds(c, 256, stride=3), :] = cols[:, c * 256 : (c + 1) * 256].T
    both = [rows[:, :256], rows[:, 256:]]
    out_ref[pl.ds(2, 256, stride=3), :] = jnp.concatenate(both + both, axis=0).T


HBM = pl.BlockSpec(memory_space=pltpu.HBM)
VMEM = pl.BlockSpec(memory_space=pltpu.VMEM)


def pack_profiles(row_profile, col_profile, send_list):
    return pl.pallas_call(
        pack_kernel,
        out_shape=(
            jax.ShapeDtypeStruct((768, 128), I32),
            jax.ShapeDtypeStruct((16, 512), I32),
            jax.ShapeDtypeStruct((16, 512), I32),
        ),
        in_specs=[HBM, HBM, VMEM],
        scratch_shapes=[
            pltpu.VMEM((BH, CELL_DEV), BF16),
            pltpu.VMEM((BW, CELL_DEV), BF16),
            pltpu.VMEM((320, 256), BF16),
            pltpu.VMEM((128, 512), I32),
            pltpu.VMEM((32, 512), I32),
            pltpu.SemaphoreType.DMA((2,)),
        ],
        compiler_params=pltpu.CompilerParams(vmem_limit_bytes=32 << 20),
        name="pack_profiles",
    )(row_profile, col_profile, send_list.T)


def slot_address(slots, core):
    source = slots // 16
    low = source // 8 * 4 + source % 4
    high = (((source // 4) % 2) ^ core) * 16 + slots % 16
    return low, high


def spread_kernel(
    own_ref,
    other_ref,
    list_hbm,
    row_hbm,
    col_hbm,
    mask_hbm,
    first_top_hbm,
    first_rest_hbm,
    turn_cos_hbm,
    turn_sin_hbm,
    second_top_hbm,
    second_rest_hbm,
    out_ref,
    wide_ref,
    tall_ref,
    low_ref,
    high_ref,
    list_ref,
    row_ref,
    col_ref,
    mask_ref,
    first_top,
    first_rest,
    turn_cos,
    turn_sin,
    second_top,
    second_rest,
    table,
    density,
    sems,
):
    core = lax.axis_index("c")
    copies = load_all(
        [
            (list_hbm, list_ref),
            (row_hbm, row_ref),
            (col_hbm, col_ref),
            (mask_hbm, mask_ref),
            (first_top_hbm, first_top),
            (first_rest_hbm, first_rest),
            (turn_cos_hbm, turn_cos),
            (turn_sin_hbm, turn_sin),
            (second_top_hbm, second_top),
            (second_rest_hbm, second_rest),
        ],
        sems,
    )
    for s, ref in enumerate((own_ref, other_ref)):
        words = ref[pl.ds(s, 256, stride=3), :].T
        for part, piece in enumerate((words & 0xFFFF, words >> 16)):
            start = s * 256 + part * 128
            table[start : start + 128, :] = (piece.astype(F32) * (1.0 / SCALE)).astype(BF16)
    own_rows = own_ref[pl.ds(2, 256, stride=3), :].T
    other_rows = other_ref[pl.ds(2, 256, stride=3), :].T
    words = jnp.concatenate([own_rows[:32], other_rows[32:64]], axis=0)
    for part, piece in enumerate((words & 0xFFFF, words >> 16)):
        start = 512 + part * 64
        table[start : start + 64, :] = (piece.astype(F32) * (1.0 / SCALE)).astype(BF16)
    for copy in copies[:4]:
        copy.wait()
    low, high = slot_address(list_ref[...], core)
    low_ref[...] = low
    high_ref[...] = high
    upper = lax.broadcasted_iota(I32, (8, TCAP), 0) // 4
    zero = jnp.zeros((8, TCAP), F32)

    def tile(t):
        found = dot(table[...], one_hot(low_ref[pl.ds(t, 1), :], LOW))
        place = jnp.broadcast_to(high_ref[pl.ds(t, 1), :], (8, TCAP))
        strip = [
            choose([found[h * 16 + s * 8 : h * 16 + s * 8 + 8] for h in range(32)], place)
            for s in range(2)
        ] + [zero]
        row_blocks = []
        for s in range(2):
            for part in range(2):
                for j in range(4):
                    start = 512 + part * 64 + s * 32 + j * 8
                    row_blocks.append(found[start : start + 8])
        row_sum = choose(row_blocks, place // 2)
        row_sum = jnp.where(place % 2 == upper, row_sum, pltpu.roll(row_sum, 4, 0))
        tall = jnp.where(upper == 0, row_sum, 0.0)
        row_shift = jnp.broadcast_to(row_ref[pl.ds(t, 1), :], (8, TCAP))
        for shift in (1, 2, 4):
            tall = jnp.where((row_shift & shift) != 0, pltpu.roll(tall, shift, 0), tall)
        col_shift = jnp.broadcast_to(col_ref[pl.ds(t, 1), :], (8, TCAP))
        for shift in (1, 2, 4):
            moves = (col_shift & shift) != 0
            moved = pltpu.roll(jnp.concatenate(strip, axis=0), shift, 0)
            strip = [jnp.where(moves, moved[i * 8 : i * 8 + 8], strip[i]) for i in range(3)]
        blocks = strip
        for shift in (1, 2, 4, 8):
            moves = (col_shift & (8 * shift)) != 0
            held = blocks
            blocks = []
            for i in range(min(16, len(held) + shift)):
                stay = held[i] if i < len(held) else zero
                come = held[i - shift] if i >= shift else zero
                blocks.append(jnp.where(moves, come, stay))
        return tall, jnp.concatenate(blocks, axis=0).astype(BF16)

    def step(group, carry):
        made = [tile(group * SPREAD_GROUP + i) for i in range(SPREAD_GROUP)]
        for i, (tall, wide) in enumerate(made):
            t = group * SPREAD_GROUP + i
            wide_ref[pl.ds(pl.multiple_of(t * 128, 128), 128), :] = wide
            tall_ref[pl.ds(pl.multiple_of(t * 8, 8), 8), :] = tall
            covered = mask_ref[:, pl.ds(pl.multiple_of(t * 128, 128), 128)].astype(F32)
            density[pl.ds(pl.multiple_of(t * 8, 8), 8), :] = (
                dot_last(tall.astype(BF16), wide) + MACRO_LEVEL * covered
            )
        return carry

    lax.fori_loop(0, NT // SPREAD_GROUP, step, 0)
    for copy in copies[4:]:
        copy.wait()
    turned = halves(density[...].T)
    mixed = dot3(turned, (first_top[...], first_rest[...]))
    real, imag = mixed[:, :512], mixed[:, 512:]
    cos, sin = turn_cos[...], turn_sin[...]
    stacked = jnp.concatenate([real * cos + imag * sin, imag * cos - real * sin], axis=0)
    result = dot3((second_top[...], second_rest[...]), halves(stacked))
    for q in range(4):
        out_ref[q * 64 : q * 64 + 64, :] = result[:, q * 128 : q * 128 + 128]


def spread(own, other, tile_list, row_offset, col_offset, macro_mask):
    first, cos, sin, second = tables_x()
    loaded = (tile_list, row_offset, col_offset, macro_mask, *first, cos, sin, *second)
    return pl.pallas_call(
        spread_kernel,
        out_shape=(
            jax.ShapeDtypeStruct((256, 128), F32),
            jax.ShapeDtypeStruct((NT * TW, TCAP), BF16),
            jax.ShapeDtypeStruct((NT * TH, TCAP), F32),
            jax.ShapeDtypeStruct((NT, TCAP), I32),
            jax.ShapeDtypeStruct((NT, TCAP), I32),
        ),
        in_specs=[VMEM, VMEM] + [HBM] * len(loaded),
        scratch_shapes=[pltpu.VMEM(array.shape, array.dtype) for array in loaded]
        + [
            pltpu.VMEM((640, 256), BF16),
            pltpu.VMEM((NT * TH, TW), F32),
            pltpu.SemaphoreType.DMA((len(loaded),)),
        ],
        compiler_params=pltpu.CompilerParams(vmem_limit_bytes=40 << 20),
        name="spread",
    )(own, other, *loaded)


def solve_kernel(
    own_ref,
    other_ref,
    first_top,
    first_rest,
    back_top,
    back_rest,
    turn_cos,
    turn_sin,
    second_top,
    second_rest,
    wave_top,
    wave_rest,
    out_ref,
    held,
):
    core = lax.axis_index("c")
    place = (lax.axis_index("x") * 16 + lax.axis_index("z")) * 4 + lax.axis_index("y")
    held[...] = join_cores(own_ref[...], other_ref[...], core)
    first = (first_top[...], first_rest[...])
    parts = []
    for h in range(4):
        mixed = dot3(first, halves(held[pl.ds(h, 64, stride=4), :]))
        real, imag = mixed[:128], mixed[128:]
        cos, sin = turn_cos[h], turn_sin[h]
        parts += [real * cos + imag * sin, imag * cos - real * sin]
    spectrum = dot3(halves(jnp.concatenate(parts, axis=1)), (second_top[...], second_rest[...]))
    lane = lax.broadcasted_iota(I32, (128, 256), 1)
    wave_u = lax.broadcasted_iota(I32, (128, 256), 0) + 128 * (lane // 8)
    wave_v = (place // 64) * 16 + core * 8 + lane % 8 + 64 * (place % 64)
    freq_u = wave_u.astype(F32) * (math.pi / GRID)
    freq_v = wave_v.astype(F32) * (math.pi / GRID)
    radius = freq_u * freq_u + freq_v * freq_v
    weight_u = jnp.where(wave_u == 0, 1.0 / GRID, 2.0 / GRID)
    weight_v = jnp.where(wave_v == 0, 1.0 / GRID, 2.0 / GRID)
    kernel = jnp.where(
        radius > 0, weight_u * weight_v / jnp.where(radius > 0, radius, 1.0), 0.0
    )
    scaled = spectrum * kernel
    both = jnp.concatenate([scaled * freq_v, scaled * freq_u], axis=0)
    waves = dot3(halves(both), (wave_top[...], wave_rest[...]))
    back = (back_top[...], back_rest[...])
    for h in range(4):
        cos, sin = turn_cos[h], turn_sin[h]
        maps = []
        for m in range(2):
            rows = slice(m * 128, m * 128 + 128)
            real = waves[rows, h * 256 : h * 256 + 128]
            imag = waves[rows, h * 256 + 128 : h * 256 + 256]
            out_real = real * cos - imag * sin
            out_imag = real * sin + imag * cos
            pair = [out_real, out_imag] if m == 0 else [out_imag, -out_real]
            maps.append(jnp.concatenate(pair, axis=0))
        result = dot3(back, halves(jnp.concatenate(maps, axis=1)))
        for m in range(2):
            out_ref[pl.ds(2 * h + m, 64, stride=8), :] = result[:, m * 128 : m * 128 + 128]


def solve_columns(own, other):
    first, cos, sin, second = tables_y()
    back = tuple(np.ascontiguousarray(part.T) for part in first)
    wave = tuple(np.ascontiguousarray(part.T) for part in second)
    return pl.pallas_call(
        solve_kernel,
        out_shape=jax.ShapeDtypeStruct((512, 128), F32),
        scratch_shapes=[pltpu.VMEM((256, 128), F32)],
        compiler_params=pltpu.CompilerParams(vmem_limit_bytes=40 << 20),
        name="solve_columns",
    )(own, other, *first, *back, cos, sin, *second, *wave)


def force_kernel(
    own_ref,
    other_ref,
    wide_ref,
    tall_ref,
    low_ref,
    high_ref,
    wave_top,
    wave_rest,
    turn_cos,
    turn_sin,
    last_top,
    last_rest,
    fields_ref,
    out_ref,
    held,
    field,
    total,
):
    core = lax.axis_index("c")
    held[...] = join_cores(own_ref[...], other_ref[...], core)
    columns = [
        held[pl.ds(q * 128 + m, 64, stride=2), :] for m in range(2) for q in range(4)
    ]
    waves = dot3((wave_top[...], wave_rest[...]), halves(jnp.concatenate(columns, axis=1)))
    cos, sin = turn_cos[...], turn_sin[...]
    maps = []
    for m in range(2):
        real = waves[:128, m * 512 : m * 512 + 512]
        imag = waves[128:, m * 512 : m * 512 + 512]
        out_real = real * cos - imag * sin
        out_imag = real * sin + imag * cos
        pair = [out_imag, -out_real] if m == 0 else [out_real, out_imag]
        maps.append(jnp.concatenate(pair, axis=1))
    result = dot3(halves(jnp.concatenate(maps, axis=0)), (last_top[...], last_rest[...]))
    field[...] = result.T
    total[...] = jnp.zeros_like(total)
    lines = lax.broadcasted_iota(I32, (32, TCAP), 0)

    def weights(t):
        here = pl.ds(pl.multiple_of(t * 8, 8), 8)
        tile = field[here, :]
        pair = jnp.concatenate([tile[:, :128], tile[:, 128:]], axis=0).astype(BF16)
        crossed = dot(pair, wide_ref[pl.ds(pl.multiple_of(t * 128, 128), 128), :])
        tall = tall_ref[here, :]
        chosen = lines == high_ref[pl.ds(t, 1), :]
        tops, rests = [], []
        for m in range(2):
            force = jnp.sum(crossed[m * 8 : m * 8 + 8] * tall, axis=0, keepdims=True) * (
                1.0 / (BH * BW)
            )
            top = force.astype(BF16).astype(F32)
            tops.append(jnp.where(chosen, top, 0.0))
            rests.append(jnp.where(chosen, force - top, 0.0))
        left = jnp.concatenate(tops + rests, axis=0).astype(BF16)
        return pair, left, one_hot(low_ref[pl.ds(t, 1), :], LOW)

    def step(group, carry):
        tiles = [group * FORCE_GROUP + i for i in range(FORCE_GROUP)]
        made = [weights(t) for t in tiles]
        for t, (pair, _, _) in zip(tiles, made):
            for m in range(2):
                fields_ref[m, :, pl.ds(pl.multiple_of(t * 128, 128), 128)] = pair[
                    m * 8 : m * 8 + 8
                ]
        left = jnp.concatenate([part[1] for part in made], axis=1)
        right = jnp.concatenate([part[2] for part in made], axis=1)
        total[...] += dot_last(left, right)
        return carry

    lax.fori_loop(0, NT // FORCE_GROUP, step, 0)
    summed = total[:64, :] + total[64:, :]
    out_ref[...] = jnp.concatenate([summed, summed], axis=0).T


def tile_forces(own, other, wide, tall, low, high):
    last, cos, sin, wave = tables_x()
    last = tuple(np.ascontiguousarray(part.T) for part in last)
    wave = tuple(np.ascontiguousarray(part.T) for part in wave)
    return pl.pallas_call(
        force_kernel,
        out_shape=(
            jax.ShapeDtypeStruct((2, TH, GRID), BF16),
            jax.ShapeDtypeStruct((256, 128), F32),
        ),
        scratch_shapes=[
            pltpu.VMEM((512, 128), F32),
            pltpu.VMEM((256, 256), F32),
            pltpu.VMEM((128, 256), F32),
        ],
        compiler_params=pltpu.CompilerParams(vmem_limit_bytes=40 << 20),
        name="tile_forces",
    )(own, other, wide, tall, low, high, *wave, cos, sin, *last)


def gather_kernel(own_ref, other_ref, low_ref, high_ref, out_ref, own, other, total):
    own[...] = own_ref[...].T
    other[...] = other_ref[...].T
    total[...] = jnp.zeros_like(total)
    lines = lax.broadcasted_iota(I32, (16, 512), 0)

    def weights(k):
        chosen = lines == high_ref[pl.ds(k, 1), :]
        tops, rests = [], []
        for m in range(2):
            force = jnp.concatenate(
                [own[pl.ds(m * 32 + k, 1), :], other[pl.ds(m * 32 + 16 + k, 1), :]], axis=1
            )
            top = force.astype(BF16).astype(F32)
            tops.append(jnp.where(chosen, top, 0.0))
            rests.append(jnp.where(chosen, force - top, 0.0))
        left = jnp.concatenate(tops + rests, axis=0).astype(BF16)
        return left, one_hot(low_ref[pl.ds(k, 1), :], LOW)

    def step(group, carry):
        made = [weights(group * GATHER_GROUP + i) for i in range(GATHER_GROUP)]
        left = jnp.concatenate([part[0] for part in made], axis=1)
        right = jnp.concatenate([part[1] for part in made], axis=1)
        total[...] += dot_last(left, right)
        return carry

    lax.fori_loop(0, CAP // GATHER_GROUP, step, 0)
    summed = total[:32, :] + total[32:, :]
    for m in range(2):
        for h in range(16):
            out_ref[m : m + 1, h * LOW : (h + 1) * LOW] = summed[m * 16 + h : m * 16 + h + 1]


def gather_forces(own, other, low, high):
    return pl.pallas_call(
        gather_kernel,
        out_shape=jax.ShapeDtypeStruct((2, CELL_DEV), F32),
        scratch_shapes=[
            pltpu.VMEM((128, 256), F32),
            pltpu.VMEM((128, 256), F32),
            pltpu.VMEM((64, 256), F32),
        ],
        compiler_params=pltpu.CompilerParams(vmem_limit_bytes=32 << 20),
        name="gather_forces",
    )(own, other, low, high)


def exchange(words):
    rows = words.shape[0]
    sent = words.reshape(256, 1, rows // 256 * 128)
    own = lax.all_to_all(sent, ("x", "z", "y"), split_axis=0, concat_axis=0, tiled=True)
    own = own.reshape(rows, 128)
    return own, lax.ppermute(own, "c", [(0, 1), (1, 0)])


def per_device(row_profile, col_profile, send_list, tile_list, row_offset, col_offset, macro_mask):
    words, cell_low, cell_high = pack_profiles(row_profile, col_profile, send_list)
    own, other = exchange(words)
    lines, wide, tall, slot_low, slot_high = spread(
        own, other, tile_list, row_offset, col_offset, macro_mask
    )
    maps = solve_columns(*exchange(lines))
    fields, forces = tile_forces(*exchange(maps), wide, tall, slot_low, slot_high)
    cell_force = gather_forces(*exchange(forces), cell_low, cell_high)
    return (fields, cell_force)


def solution(mesh):
    fine = Mesh(mesh.devices.reshape(4, 16, 2, 4), ("x", "z", "c", "y"))
    every = ("x", "z", "c", "y")
    placed = (P(None, every), P(None, every)) + (P(every, None),) * 5
    return jax.shard_map(
        per_device,
        mesh=fine,
        in_specs=placed,
        out_specs=(P(None, every, None), P(None, every)),
        check_vma=False,
    )
```

```python
import functools
import math

import jax
import jax.numpy as jnp
import numpy as np
from jax import lax
from jax.experimental import pallas as pl
from jax.experimental.pallas import tpu as pltpu
from jax.sharding import Mesh
from jax.sharding import PartitionSpec as P

GRID = 4096
BH = 4
BW = 16
TW = 128
TH = 8
NT = 32
TCAP = 256
CAP = 16
CELL_DEV = 4096
LOW = 256
MACRO_LEVEL = 4.0
SCALE = 8192.0
OCTAVES = 25.0
STEPS = 819.0
SPREAD_GROUP = 16
FORCE_GROUP = 16
GATHER_GROUP = 16
F32 = jnp.float32
BF16 = jnp.bfloat16
I32 = jnp.int32


def split_host(values):
    top = values.astype(jnp.bfloat16)
    rest = (values - top.astype(np.float64)).astype(jnp.bfloat16)
    return top, rest


@functools.cache
def tables_x():
    q = np.arange(512) // 128
    r = (np.arange(512) % 128) // 16
    f = 16 * q + np.arange(512) % 16
    t = np.arange(256) // 8
    r_in = np.arange(256) % 8
    same = r_in[:, None] == r[None, :]
    turn = np.pi * ((t[:, None] * f[None, :]) % 64) / 32.0
    first = np.concatenate([np.cos(turn) * same, -np.sin(turn) * same], axis=1)
    b = np.arange(128)
    angle = np.pi * (f[None, :] * (2 * b[:, None] + 1)) / 8192.0
    w = np.arange(64)
    wave = np.pi * ((w[:, None] * (2 * b[None, :] + 1)) % 256) / 128.0
    second = np.concatenate([np.cos(wave), np.sin(wave)], axis=1)
    return (
        split_host(first),
        np.cos(angle).astype(np.float32),
        np.sin(angle).astype(np.float32),
        split_host(second),
    )


@functools.cache
def tables_y():
    lane = np.arange(128)
    r, g = lane // 16, lane % 16
    f = np.arange(128)
    a = np.arange(64)
    a = a % 4 * 16 + a // 4
    turn = np.pi * ((f[:, None] * a[None, :]) % 128) / 64.0
    first = np.concatenate([np.cos(turn), -np.sin(turn)], axis=0)
    b = 8 * np.arange(8)[:, None] + r[None, :]
    angle = np.pi * (f[None, :, None] * (2 * b[:, None, :] + 1)) / 8192.0
    w = np.arange(512) // 16
    wave = np.pi * (((2 * b[:4, :, None] + 1) * w[None, None, :]) % 128) / 64.0
    same = g[:, None] == (np.arange(512) % 16)[None, :]
    second = np.stack([np.cos(wave) * same[None], np.sin(wave) * same[None]], axis=1)
    return (
        split_host(first),
        np.cos(angle).astype(np.float32),
        np.sin(angle).astype(np.float32),
        split_host(second.reshape(1024, 512)),
    )


def halves(values):
    top = values.astype(BF16)
    return top, (values - top.astype(F32)).astype(BF16)


def dot(left, right):
    return jnp.dot(left, right, preferred_element_type=F32)


def dot_last(left, right):
    return lax.dot_general(left, right, (((1,), (1,)), ((), ())), preferred_element_type=F32)


def dot3(left, right):
    left_top, left_rest = left
    right_top, right_rest = right
    return dot(left_top, right_top) + (dot(left_rest, right_top) + dot(left_top, right_rest))


def one_hot(index_row, extent):
    shape = (extent, index_row.shape[1])
    lines = lax.broadcasted_iota(I32, shape, 0).astype(BF16)
    index = jnp.broadcast_to(index_row.astype(BF16), shape)
    return jnp.where(lines == index, jnp.ones(shape, BF16), jnp.zeros(shape, BF16))


def choose(blocks, index):
    bit = 1
    while len(blocks) > 1:
        odd = (index & bit) != 0
        blocks = [
            jnp.where(odd, blocks[2 * i + 1], blocks[2 * i]) for i in range(len(blocks) // 2)
        ]
        bit *= 2
    return blocks[0]


def load_all(pairs, sems):
    copies = [
        pltpu.make_async_copy(source, target, sems.at[i])
        for i, (source, target) in enumerate(pairs)
    ]
    for copy in copies:
        copy.start()
    return copies


def encode(values):
    size = jnp.abs(values)
    level = (jnp.log(jnp.maximum(size, 2.0**-30)) * (1.0 / math.log(2.0)) + OCTAVES) * STEPS
    level = jnp.clip(jnp.floor(level + 0.5), 0.0, 32767.0).astype(I32)
    return level + jnp.where(values < 0, 32768, 0)


def decode(codes):
    level = codes & 0x7FFF
    size = jnp.exp((level.astype(F32) * (1.0 / STEPS) - OCTAVES) * math.log(2.0))
    size = jnp.where(level == 0, 0.0, size)
    return jnp.where((codes & 0x8000) != 0, -size, size)


def pack_kernel(
    row_hbm,
    col_hbm,
    list_hbm,
    out_ref,
    low_ref,
    high_ref,
    row_ref,
    col_ref,
    list_ref,
    table,
    cols,
    rows,
    sems,
):
    core = lax.axis_index("c")
    copies = load_all([(list_hbm, list_ref), (col_hbm, col_ref), (row_hbm, row_ref)], sems)
    copies[0].wait()
    listed = list_ref[...].astype(F32)
    empty = listed >= CELL_DEV
    high = jnp.floor(listed * (1.0 / LOW))
    low = jnp.where(empty, float(LOW), listed - high * LOW)
    target = lax.broadcasted_iota(I32, (512, 512), 1)
    chip = target // 4 % 4 * 16 + target // 16 % 16
    source = chip * 8 + ((target // 256) ^ core) * 4 + target % 4
    move = jnp.where(lax.broadcasted_iota(I32, (512, 512), 0) == source, 1.0, 0.0).astype(BF16)
    high_ref[...] = dot(high.astype(BF16), move).astype(I32)
    low_ref[...] = dot(low.astype(BF16), move).astype(I32)
    for copy in copies[1:]:
        copy.wait()
    for h in range(16):
        table[h * 16 : h * 16 + 16, :] = col_ref[:, h * LOW : (h + 1) * LOW]
    table[256:320, :] = jnp.concatenate(
        [row_ref[:, h * LOW : (h + 1) * LOW].astype(F32) for h in range(16)], axis=0
    ).astype(BF16)
    upper = lax.broadcasted_iota(I32, (8, 512), 0) // 4

    def pick(k):
        found = dot(table[...], one_hot(low_ref[pl.ds(k, 1), :], LOW))
        place = jnp.broadcast_to(high_ref[pl.ds(k, 1), :], (8, 512))
        col_sum = jnp.concatenate(
            [
                choose([found[h * 16 + s * 8 : h * 16 + s * 8 + 8] for h in range(16)], place)
                for s in range(2)
            ],
            axis=0,
        )
        row_sum = choose([found[256 + h * 8 : 264 + h * 8] for h in range(8)], place // 2)
        row_sum = jnp.where(place % 2 == upper, row_sum, pltpu.roll(row_sum, 4, 0))
        return (col_sum * SCALE).astype(I32), (row_sum * SCALE).astype(I32)

    def step(j, carry):
        row_words = []
        for s in range(2):
            k = 2 * j + s
            col_a, row_a = pick(k)
            col_b, row_b = pick(k + 8)
            cols[pl.ds(pl.multiple_of(k * 16, 16), 16), :] = col_a + (col_b << 16)
            row_words.append(row_a + (row_b << 16))
        rows[pl.ds(pl.multiple_of(j * 8, 8), 8), :] = jnp.where(
            upper == 0, row_words[0], pltpu.roll(row_words[1], 4, 0)
        )
        return carry

    lax.fori_loop(0, 4, step, 0, unroll=True)
    for c in range(2):
        out_ref[pl.ds(c, 256, stride=3), :] = cols[:, c * 256 : (c + 1) * 256].T
    both = [rows[:, :256], rows[:, 256:]]
    out_ref[pl.ds(2, 256, stride=3), :] = jnp.concatenate(both + both, axis=0).T


HBM = pl.BlockSpec(memory_space=pltpu.HBM)
VMEM = pl.BlockSpec(memory_space=pltpu.VMEM)


def pack_profiles(row_profile, col_profile, send_list):
    return pl.pallas_call(
        pack_kernel,
        out_shape=(
            jax.ShapeDtypeStruct((768, 128), I32),
            jax.ShapeDtypeStruct((16, 512), I32),
            jax.ShapeDtypeStruct((16, 512), I32),
        ),
        in_specs=[HBM, HBM, HBM],
        scratch_shapes=[
            pltpu.VMEM((BH, CELL_DEV), BF16),
            pltpu.VMEM((BW, CELL_DEV), BF16),
            pltpu.VMEM((CAP, 512), I32),
            pltpu.VMEM((320, 256), BF16),
            pltpu.VMEM((128, 512), I32),
            pltpu.VMEM((32, 512), I32),
            pltpu.SemaphoreType.DMA((3,)),
        ],
        compiler_params=pltpu.CompilerParams(vmem_limit_bytes=60 << 20),
        cost_estimate=pl.CostEstimate(flops=15000000000, bytes_accessed=10000000, transcendentals=0),
        name="pack_profiles",
    )(row_profile, col_profile, send_list.T)


def slot_address(slots, core):
    source = slots // 16
    low = source // 8 % 16 * 16 + source // 128 * 4 + source % 4
    low = jnp.where(source < 512, low, LOW)
    high = (((source // 4) % 2) ^ core) * 16 + slots % 16
    return low, high


def spread_kernel(
    own_ref,
    other_ref,
    list_hbm,
    row_hbm,
    col_hbm,
    mask_hbm,
    first_top_hbm,
    first_rest_hbm,
    turn_cos_hbm,
    turn_sin_hbm,
    second_top_hbm,
    second_rest_hbm,
    out_ref,
    wide_ref,
    tall_ref,
    low_ref,
    high_ref,
    list_ref,
    row_ref,
    col_ref,
    mask_ref,
    first_top,
    first_rest,
    turn_cos,
    turn_sin,
    second_top,
    second_rest,
    table,
    density,
    sems,
):
    core = lax.axis_index("c")
    copies = load_all(
        [
            (list_hbm, list_ref),
            (row_hbm, row_ref),
            (col_hbm, col_ref),
            (mask_hbm, mask_ref),
            (first_top_hbm, first_top),
            (first_rest_hbm, first_rest),
            (turn_cos_hbm, turn_cos),
            (turn_sin_hbm, turn_sin),
            (second_top_hbm, second_top),
            (second_rest_hbm, second_rest),
        ],
        sems,
    )
    for s, ref in enumerate((own_ref, other_ref)):
        words = ref[pl.ds(s, 256, stride=3), :].T
        for part, piece in enumerate((words & 0xFFFF, words >> 16)):
            start = s * 256 + part * 128
            table[start : start + 128, :] = (piece.astype(F32) * (1.0 / SCALE)).astype(BF16)
    own_rows = own_ref[pl.ds(2, 256, stride=3), :].T
    other_rows = other_ref[pl.ds(2, 256, stride=3), :].T
    words = jnp.concatenate([own_rows[:32], other_rows[32:64]], axis=0)
    for part, piece in enumerate((words & 0xFFFF, words >> 16)):
        start = 512 + part * 64
        table[start : start + 64, :] = (piece.astype(F32) * (1.0 / SCALE)).astype(BF16)
    for copy in copies[:4]:
        copy.wait()
    low, high = slot_address(list_ref[...], core)
    low_ref[...] = low
    high_ref[...] = high
    upper = lax.broadcasted_iota(I32, (8, TCAP), 0) // 4
    zero = jnp.zeros((8, TCAP), F32)

    def tile(t):
        found = dot(table[...], one_hot(low_ref[pl.ds(t, 1), :], LOW))
        place = jnp.broadcast_to(high_ref[pl.ds(t, 1), :], (8, TCAP))
        strip = [
            choose([found[h * 16 + s * 8 : h * 16 + s * 8 + 8] for h in range(32)], place)
            for s in range(2)
        ] + [zero]
        row_blocks = []
        for s in range(2):
            for part in range(2):
                for j in range(4):
                    start = 512 + part * 64 + s * 32 + j * 8
                    row_blocks.append(found[start : start + 8])
        row_sum = choose(row_blocks, place // 2)
        row_sum = jnp.where(place % 2 == upper, row_sum, pltpu.roll(row_sum, 4, 0))
        tall = jnp.where(upper == 0, row_sum, 0.0)
        row_shift = jnp.broadcast_to(row_ref[pl.ds(t, 1), :], (8, TCAP))
        for shift in (1, 2, 4):
            tall = jnp.where((row_shift & shift) != 0, pltpu.roll(tall, shift, 0), tall)
        col_shift = jnp.broadcast_to(col_ref[pl.ds(t, 1), :], (8, TCAP))
        for shift in (1, 2, 4):
            moves = (col_shift & shift) != 0
            moved = pltpu.roll(jnp.concatenate(strip, axis=0), shift, 0)
            strip = [jnp.where(moves, moved[i * 8 : i * 8 + 8], strip[i]) for i in range(3)]
        blocks = strip
        for shift in (1, 2, 4, 8):
            moves = (col_shift & (8 * shift)) != 0
            held = blocks
            blocks = []
            for i in range(min(16, len(held) + shift)):
                stay = held[i] if i < len(held) else zero
                come = held[i - shift] if i >= shift else zero
                blocks.append(jnp.where(moves, come, stay))
        return tall, jnp.concatenate(blocks, axis=0).astype(BF16)

    def step(group, carry):
        made = [tile(group * SPREAD_GROUP + i) for i in range(SPREAD_GROUP)]
        for i, (tall, wide) in enumerate(made):
            t = group * SPREAD_GROUP + i
            wide_ref[pl.ds(pl.multiple_of(t * 128, 128), 128), :] = wide
            tall_ref[pl.ds(pl.multiple_of(t * 8, 8), 8), :] = tall
            covered = mask_ref[:, pl.ds(pl.multiple_of(t * 128, 128), 128)].astype(F32)
            density[pl.ds(pl.multiple_of(t * 8, 8), 8), :] = (
                dot_last(tall.astype(BF16), wide) + MACRO_LEVEL * covered
            )
        return carry

    lax.fori_loop(0, NT // SPREAD_GROUP, step, 0)
    for copy in copies[4:]:
        copy.wait()
    turned = halves(density[...].T)
    mixed = dot3(turned, (first_top[...], first_rest[...]))
    real, imag = mixed[:, :512], mixed[:, 512:]
    cos, sin = turn_cos[...], turn_sin[...]
    stacked = jnp.concatenate([real * cos + imag * sin, imag * cos - real * sin], axis=0)
    result = dot3((second_top[...], second_rest[...]), halves(stacked))
    for q in range(4):
        out_ref[q * 64 : q * 64 + 64, :] = result[:, q * 128 : q * 128 + 128]


def spread(own, other, tile_list, row_offset, col_offset, macro_mask):
    first, cos, sin, second = tables_x()
    loaded = (tile_list, row_offset, col_offset, macro_mask, *first, cos, sin, *second)
    return pl.pallas_call(
        spread_kernel,
        out_shape=(
            jax.ShapeDtypeStruct((256, 128), F32),
            jax.ShapeDtypeStruct((NT * TW, TCAP), BF16),
            jax.ShapeDtypeStruct((NT * TH, TCAP), F32),
            jax.ShapeDtypeStruct((NT, TCAP), I32),
            jax.ShapeDtypeStruct((NT, TCAP), I32),
        ),
        in_specs=[VMEM, VMEM] + [HBM] * len(loaded),
        scratch_shapes=[pltpu.VMEM(array.shape, array.dtype) for array in loaded]
        + [
            pltpu.VMEM((640, 256), BF16),
            pltpu.VMEM((NT * TH, TW), F32),
            pltpu.SemaphoreType.DMA((len(loaded),)),
        ],
        compiler_params=pltpu.CompilerParams(vmem_limit_bytes=40 << 20),
        cost_estimate=pl.CostEstimate(flops=60000000000, bytes_accessed=30000000, transcendentals=0),
        name="spread",
    )(own, other, *loaded)


def column_kernel(
    got_ref, first_top, first_rest, turn_cos, turn_sin, second_top, second_rest, out_ref
):
    core = lax.axis_index("c")
    first = (first_top[...], first_rest[...])
    parts = []
    for h in range(4):
        mixed = dot3(first, halves(got_ref[pl.ds(h, 64, stride=4), :]))
        real, imag = mixed[:128], mixed[128:]
        cos, sin = turn_cos[core * 4 + h], turn_sin[core * 4 + h]
        parts += [real * cos + imag * sin, imag * cos - real * sin]
    partial = dot3(halves(jnp.concatenate(parts, axis=1)), (second_top[...], second_rest[...]))
    odd = (lax.broadcasted_iota(I32, (128, 512), 1) // 16) % 2
    out_ref[...] = jnp.where(odd * core == 1, -partial, partial)


def transform_columns(got):
    first, cos, sin, second = tables_y()
    return pl.pallas_call(
        column_kernel,
        out_shape=jax.ShapeDtypeStruct((128, 512), F32),
        compiler_params=pltpu.CompilerParams(vmem_limit_bytes=32 << 20),
        cost_estimate=pl.CostEstimate(
            flops=20000000000, bytes_accessed=20000000, transcendentals=0
        ),
        name="transform_columns",
    )(got, *first, cos, sin, *second)


def solve_kernel(
    own_ref,
    other_ref,
    back_top,
    back_rest,
    turn_cos,
    turn_sin,
    wave_top,
    wave_rest,
    out_ref,
):
    core = lax.axis_index("c")
    place = (lax.axis_index("z") * 4 + lax.axis_index("x")) * 4 + lax.axis_index("y")
    lane = lax.broadcasted_iota(I32, (128, 512), 1)
    wave_u = lax.broadcasted_iota(I32, (128, 512), 0) + 128 * (lane // 16)
    wave_v = (place // 64) * 16 + lane % 16 + 64 * (place % 64)
    freq_u = wave_u.astype(F32) * (math.pi / GRID)
    freq_v = wave_v.astype(F32) * (math.pi / GRID)
    radius = freq_u * freq_u + freq_v * freq_v
    weight_u = jnp.where(wave_u == 0, 1.0 / GRID, 2.0 / GRID)
    weight_v = jnp.where(wave_v == 0, 1.0 / GRID, 2.0 / GRID)
    kernel = jnp.where(
        radius > 0, weight_u * weight_v / jnp.where(radius > 0, radius, 1.0), 0.0
    )
    kernel = jnp.where((lane // 16) % 2 * core == 1, -kernel, kernel)
    scaled = (own_ref[...] + other_ref[...]) * kernel
    both = jnp.concatenate([scaled * freq_v, scaled * freq_u], axis=0)
    waves = dot3(halves(both), (wave_top[...], wave_rest[...]))
    back = (back_top[...], back_rest[...])
    for h in range(4):
        cos, sin = turn_cos[core * 4 + h], turn_sin[core * 4 + h]
        maps = []
        for m in range(2):
            rows = slice(m * 128, m * 128 + 128)
            real = waves[rows, h * 256 : h * 256 + 128]
            imag = waves[rows, h * 256 + 128 : h * 256 + 256]
            out_real = real * cos - imag * sin
            out_imag = real * sin + imag * cos
            pair = [out_real, out_imag] if m == 0 else [out_imag, -out_real]
            maps.append(jnp.concatenate(pair, axis=0))
        codes = encode(dot3(back, halves(jnp.concatenate(maps, axis=1))))
        out_ref[pl.ds(h, 64, stride=4), :] = codes[:, :128] + (codes[:, 128:] << 16)


def solve_columns(own, other):
    first, cos, sin, second = tables_y()
    back = tuple(np.ascontiguousarray(part.T) for part in first)
    wave = tuple(np.ascontiguousarray(part.T) for part in second)
    return pl.pallas_call(
        solve_kernel,
        out_shape=jax.ShapeDtypeStruct((256, 128), I32),
        compiler_params=pltpu.CompilerParams(vmem_limit_bytes=32 << 20),
        cost_estimate=pl.CostEstimate(
            flops=20000000000, bytes_accessed=20000000, transcendentals=0
        ),
        name="solve_columns",
    )(own, other, *back, cos, sin, *wave)


def force_kernel(
    got_ref,
    wide_ref,
    tall_ref,
    low_ref,
    high_ref,
    wave_top,
    wave_rest,
    turn_cos,
    turn_sin,
    last_top,
    last_rest,
    fields_ref,
    out_ref,
    field,
    total,
):
    codes = got_ref[...]
    maps = [decode(codes), decode(codes >> 16)]
    columns = [maps[m][q * 64 : q * 64 + 64] for m in range(2) for q in range(4)]
    waves = dot3((wave_top[...], wave_rest[...]), halves(jnp.concatenate(columns, axis=1)))
    cos, sin = turn_cos[...], turn_sin[...]
    maps = []
    for m in range(2):
        real = waves[:128, m * 512 : m * 512 + 512]
        imag = waves[128:, m * 512 : m * 512 + 512]
        out_real = real * cos - imag * sin
        out_imag = real * sin + imag * cos
        pair = [out_imag, -out_real] if m == 0 else [out_real, out_imag]
        maps.append(jnp.concatenate(pair, axis=1))
    result = dot3(halves(jnp.concatenate(maps, axis=0)), (last_top[...], last_rest[...]))
    field[...] = result.T
    total[...] = jnp.zeros_like(total)
    lines = lax.broadcasted_iota(I32, (32, TCAP), 0)

    def weights(t):
        here = pl.ds(pl.multiple_of(t * 8, 8), 8)
        tile = field[here, :]
        pair = jnp.concatenate([tile[:, :128], tile[:, 128:]], axis=0).astype(BF16)
        crossed = dot(pair, wide_ref[pl.ds(pl.multiple_of(t * 128, 128), 128), :])
        tall = tall_ref[here, :]
        chosen = lines == high_ref[pl.ds(t, 1), :]
        tops, rests = [], []
        for m in range(2):
            force = jnp.sum(crossed[m * 8 : m * 8 + 8] * tall, axis=0, keepdims=True) * (
                1.0 / (BH * BW)
            )
            top = force.astype(BF16).astype(F32)
            tops.append(jnp.where(chosen, top, 0.0))
            rests.append(jnp.where(chosen, force - top, 0.0))
        left = jnp.concatenate(tops + rests, axis=0).astype(BF16)
        return pair, left, one_hot(low_ref[pl.ds(t, 1), :], LOW)

    def step(group, carry):
        tiles = [group * FORCE_GROUP + i for i in range(FORCE_GROUP)]
        made = [weights(t) for t in tiles]
        for t, (pair, _, _) in zip(tiles, made):
            for m in range(2):
                fields_ref[m, :, pl.ds(pl.multiple_of(t * 128, 128), 128)] = pair[
                    m * 8 : m * 8 + 8
                ]
        left = jnp.concatenate([part[1] for part in made], axis=1)
        right = jnp.concatenate([part[2] for part in made], axis=1)
        total[...] += dot_last(left, right)
        return carry

    lax.fori_loop(0, NT // FORCE_GROUP, step, 0)
    summed = total[:64, :] + total[64:, :]
    out_ref[...] = jnp.concatenate([summed, summed], axis=0).T


def tile_forces(got, wide, tall, low, high):
    last, cos, sin, wave = tables_x()
    last = tuple(np.ascontiguousarray(part.T) for part in last)
    wave = tuple(np.ascontiguousarray(part.T) for part in wave)
    return pl.pallas_call(
        force_kernel,
        out_shape=(
            jax.ShapeDtypeStruct((2, TH, GRID), BF16),
            jax.ShapeDtypeStruct((256, 128), F32),
        ),
        scratch_shapes=[
            pltpu.VMEM((256, 256), F32),
            pltpu.VMEM((128, 256), F32),
        ],
        compiler_params=pltpu.CompilerParams(vmem_limit_bytes=40 << 20),
        cost_estimate=pl.CostEstimate(flops=40000000000, bytes_accessed=30000000, transcendentals=0),
        name="tile_forces",
    )(got, wide, tall, low, high, *wave, cos, sin, *last)


def gather_kernel(own_ref, other_ref, low_ref, high_ref, out_ref, own, other, total):
    own[...] = own_ref[...].T
    other[...] = other_ref[...].T
    total[...] = jnp.zeros_like(total)
    lines = lax.broadcasted_iota(I32, (16, 512), 0)

    def weights(k):
        chosen = lines == high_ref[pl.ds(k, 1), :]
        tops, rests = [], []
        for m in range(2):
            force = jnp.concatenate(
                [own[pl.ds(m * 32 + k, 1), :], other[pl.ds(m * 32 + 16 + k, 1), :]], axis=1
            )
            top = force.astype(BF16).astype(F32)
            tops.append(jnp.where(chosen, top, 0.0))
            rests.append(jnp.where(chosen, force - top, 0.0))
        left = jnp.concatenate(tops + rests, axis=0).astype(BF16)
        return left, one_hot(low_ref[pl.ds(k, 1), :], LOW)

    def step(group, carry):
        made = [weights(group * GATHER_GROUP + i) for i in range(GATHER_GROUP)]
        left = jnp.concatenate([part[0] for part in made], axis=1)
        right = jnp.concatenate([part[1] for part in made], axis=1)
        total[...] += dot_last(left, right)
        return carry

    lax.fori_loop(0, CAP // GATHER_GROUP, step, 0)
    summed = total[:32, :] + total[32:, :]
    for m in range(2):
        for h in range(16):
            out_ref[m : m + 1, h * LOW : (h + 1) * LOW] = summed[m * 16 + h : m * 16 + h + 1]


def gather_forces(own, other, low, high):
    return pl.pallas_call(
        gather_kernel,
        out_shape=jax.ShapeDtypeStruct((2, CELL_DEV), F32),
        scratch_shapes=[
            pltpu.VMEM((128, 256), F32),
            pltpu.VMEM((128, 256), F32),
            pltpu.VMEM((64, 256), F32),
        ],
        compiler_params=pltpu.CompilerParams(vmem_limit_bytes=32 << 20),
        cost_estimate=pl.CostEstimate(flops=20000000000, bytes_accessed=5000000, transcendentals=0),
        name="gather_forces",
    )(own, other, low, high)


def between_chips(words):
    rows = words.shape[0]
    sent = words.reshape(256, 1, rows // 256 * 128)
    got = lax.all_to_all(sent, ("z", "x", "y"), split_axis=0, concat_axis=0, tiled=True)
    return got.reshape(rows, 128)


def with_other(own):
    return own, lax.ppermute(own, "c", [(0, 1), (1, 0)])


def per_device(row_profile, col_profile, send_list, tile_list, row_offset, col_offset, macro_mask):
    words, cell_low, cell_high = pack_profiles(row_profile, col_profile, send_list)
    own, other = with_other(between_chips(words))
    lines, wide, tall, slot_low, slot_high = spread(
        own, other, tile_list, row_offset, col_offset, macro_mask
    )
    partial = transform_columns(between_chips(lines))
    maps = solve_columns(*with_other(partial))
    fields, forces = tile_forces(between_chips(maps), wide, tall, slot_low, slot_high)
    cell_force = gather_forces(*with_other(between_chips(forces)), cell_low, cell_high)
    return (fields, cell_force)


def solution(mesh):
    fine = Mesh(mesh.devices.reshape(4, 16, 2, 4), ("x", "z", "c", "y"))
    every = ("x", "z", "c", "y")
    placed = (P(None, every), P(None, every)) + (P(every, None),) * 5
    return jax.shard_map(
        per_device,
        mesh=fine,
        in_specs=placed,
        out_specs=(P(None, every, None), P(None, every)),
        check_vma=False,
    )
```

```python
import functools
import math

import jax
import jax.numpy as jnp
import numpy as np
from jax import lax
from jax.experimental import pallas as pl
from jax.experimental.pallas import tpu as pltpu
from jax.sharding import Mesh
from jax.sharding import PartitionSpec as P

GRID = 4096
BH = 4
BW = 16
TW = 128
TH = 8
NT = 32
TCAP = 256
CAP = 16
CELL_DEV = 4096
LOW = 256
MACRO_LEVEL = 4.0
SCALE = 8192.0
OCTAVES = 25.0
STEPS = 819.0
SPREAD_GROUP = 32
FORCE_GROUP = 16
GATHER_GROUP = 16
F32 = jnp.float32
BF16 = jnp.bfloat16
I32 = jnp.int32

AXES = ("x", "z3", "z2", "z1", "z0", "c", "y")
CHIPS = ("z0", "z1", "z2", "z3", "x", "y")


def turned(z):
    return (z & 1) * 8 + (z & 2) * 2 + (z & 4) // 2 + (z & 8) // 8


def split_host(values):
    top = values.astype(jnp.bfloat16)
    rest = (values - top.astype(np.float64)).astype(jnp.bfloat16)
    return top, rest


@functools.cache
def tables_x():
    q = np.arange(512) // 128
    r = (np.arange(512) % 128) // 16
    f = 16 * q + np.arange(512) % 16
    t = np.arange(256) // 8
    r_in = np.arange(256) % 8
    same = r_in[:, None] == r[None, :]
    turn = np.pi * ((t[:, None] * f[None, :]) % 64) / 32.0
    first = np.concatenate([np.cos(turn) * same, -np.sin(turn) * same], axis=1)
    b = np.arange(128)
    angle = np.pi * (f[None, :] * (2 * b[:, None] + 1)) / 8192.0
    w = np.arange(64)
    wave = np.pi * ((w[:, None] * (2 * b[None, :] + 1)) % 256) / 128.0
    second = np.concatenate([np.cos(wave), np.sin(wave)], axis=1)
    return (
        split_host(first),
        np.cos(angle).astype(np.float32),
        np.sin(angle).astype(np.float32),
        split_host(second),
    )


@functools.cache
def tables_y():
    lane = np.arange(128)
    r, g = lane // 16, lane % 16
    f = np.arange(128)
    a = np.arange(64)
    a = a % 4 * 16 + turned(a // 4)
    turn = np.pi * ((f[:, None] * a[None, :]) % 128) / 64.0
    first = np.concatenate([np.cos(turn), -np.sin(turn)], axis=0)
    b = 8 * np.arange(8)[:, None] + r[None, :]
    angle = np.pi * (f[None, :, None] * (2 * b[:, None, :] + 1)) / 8192.0
    w = np.arange(512) // 16
    wave = np.pi * (((2 * b[:4, :, None] + 1) * w[None, None, :]) % 128) / 64.0
    same = g[:, None] == (np.arange(512) % 16)[None, :]
    second = np.stack([np.cos(wave) * same[None], np.sin(wave) * same[None]], axis=1)
    return (
        split_host(first),
        np.cos(angle).astype(np.float32),
        np.sin(angle).astype(np.float32),
        split_host(second.reshape(1024, 512)),
    )


def halves(values):
    top = values.astype(BF16)
    return top, (values - top.astype(F32)).astype(BF16)


def dot(left, right):
    return jnp.dot(left, right, preferred_element_type=F32)


def dot_last(left, right):
    return lax.dot_general(left, right, (((1,), (1,)), ((), ())), preferred_element_type=F32)


def dot3(left, right):
    left_top, left_rest = left
    right_top, right_rest = right
    return dot(left_top, right_top) + (dot(left_rest, right_top) + dot(left_top, right_rest))


def one_hot(index_row, extent):
    shape = (extent, index_row.shape[1])
    lines = lax.broadcasted_iota(I32, shape, 0).astype(BF16)
    index = jnp.broadcast_to(index_row.astype(BF16), shape)
    return jnp.where(lines == index, jnp.ones(shape, BF16), jnp.zeros(shape, BF16))


def choose(blocks, index):
    bit = 1
    while len(blocks) > 1:
        odd = (index & bit) != 0
        blocks = [
            jnp.where(odd, blocks[2 * i + 1], blocks[2 * i]) for i in range(len(blocks) // 2)
        ]
        bit *= 2
    return blocks[0]


def load_all(pairs, sems):
    copies = [
        pltpu.make_async_copy(source, target, sems.at[i])
        for i, (source, target) in enumerate(pairs)
    ]
    for copy in copies:
        copy.start()
    return copies


def encode(values):
    size = jnp.abs(values)
    level = (jnp.log(jnp.maximum(size, 2.0**-30)) * (1.0 / math.log(2.0)) + OCTAVES) * STEPS
    level = jnp.clip(jnp.floor(level + 0.5), 0.0, 32767.0).astype(I32)
    return level + jnp.where(values < 0, 32768, 0)


def decode(codes):
    level = codes & 0x7FFF
    size = jnp.exp((level.astype(F32) * (1.0 / STEPS) - OCTAVES) * math.log(2.0))
    size = jnp.where(level == 0, 0.0, size)
    return jnp.where((codes & 0x8000) != 0, -size, size)


def pack_kernel(
    row_hbm,
    col_hbm,
    list_hbm,
    out_ref,
    low_ref,
    high_ref,
    row_ref,
    col_ref,
    list_ref,
    table,
    cols,
    rows,
    sems,
):
    core = lax.axis_index("c")
    copies = load_all([(list_hbm, list_ref), (col_hbm, col_ref), (row_hbm, row_ref)], sems)
    target = lax.broadcasted_iota(I32, (1, 512), 1)
    chip = target // 4 % 4 * 16 + turned(target // 16 % 16)
    source = chip * 8 + ((target // 256) ^ core) * 4 + target % 4
    lines = lax.broadcasted_iota(I32, (512, 512), 0)
    move = jnp.where(lines == source, 1.0, 0.0).astype(BF16)
    copies[0].wait()
    listed = list_ref[...].astype(F32)
    empty = listed >= CELL_DEV
    high = jnp.floor(listed * (1.0 / LOW))
    low = jnp.where(empty, float(LOW), listed - high * LOW)
    high_ref[...] = dot(high.astype(BF16), move).astype(I32)
    low_ref[...] = dot(low.astype(BF16), move).astype(I32)
    for copy in copies[1:]:
        copy.wait()
    for h in range(16):
        table[h * 16 : h * 16 + 16, :] = col_ref[:, h * LOW : (h + 1) * LOW]
    table[256:320, :] = jnp.concatenate(
        [row_ref[:, h * LOW : (h + 1) * LOW].astype(F32) for h in range(16)], axis=0
    ).astype(BF16)
    upper = lax.broadcasted_iota(I32, (8, 512), 0) // 4

    def pick(k):
        found = dot(table[...], one_hot(low_ref[pl.ds(k, 1), :], LOW))
        place = jnp.broadcast_to(high_ref[pl.ds(k, 1), :], (8, 512))
        col_sum = jnp.concatenate(
            [
                choose([found[h * 16 + s * 8 : h * 16 + s * 8 + 8] for h in range(16)], place)
                for s in range(2)
            ],
            axis=0,
        )
        row_sum = choose([found[256 + h * 8 : 264 + h * 8] for h in range(8)], place // 2)
        row_sum = jnp.where(place % 2 == upper, row_sum, pltpu.roll(row_sum, 4, 0))
        return (col_sum * SCALE).astype(I32), (row_sum * SCALE).astype(I32)

    def step(j, carry):
        row_words = []
        for s in range(2):
            k = 2 * j + s
            col_a, row_a = pick(k)
            col_b, row_b = pick(k + 8)
            cols[pl.ds(pl.multiple_of(k * 16, 16), 16), :] = col_a + (col_b << 16)
            row_words.append(row_a + (row_b << 16))
        rows[pl.ds(pl.multiple_of(j * 8, 8), 8), :] = jnp.where(
            upper == 0, row_words[0], pltpu.roll(row_words[1], 4, 0)
        )
        return carry

    lax.fori_loop(0, 4, step, 0, unroll=True)
    for c in range(2):
        out_ref[pl.ds(c, 256, stride=3), :] = cols[:, c * 256 : (c + 1) * 256].T
    both = [rows[:, :256], rows[:, 256:]]
    out_ref[pl.ds(2, 256, stride=3), :] = jnp.concatenate(both + both, axis=0).T


HBM = pl.BlockSpec(memory_space=pltpu.HBM)
VMEM = pl.BlockSpec(memory_space=pltpu.VMEM)


def pack_profiles(row_profile, col_profile, send_list):
    return pl.pallas_call(
        pack_kernel,
        out_shape=(
            jax.ShapeDtypeStruct((768, 128), I32),
            jax.ShapeDtypeStruct((16, 512), I32),
            jax.ShapeDtypeStruct((16, 512), I32),
        ),
        in_specs=[HBM, HBM, HBM],
        scratch_shapes=[
            pltpu.VMEM((BH, CELL_DEV), BF16),
            pltpu.VMEM((BW, CELL_DEV), BF16),
            pltpu.VMEM((CAP, 512), I32),
            pltpu.VMEM((320, 256), BF16),
            pltpu.VMEM((128, 512), I32),
            pltpu.VMEM((32, 512), I32),
            pltpu.SemaphoreType.DMA((3,)),
        ],
        compiler_params=pltpu.CompilerParams(vmem_limit_bytes=60 << 20),
        cost_estimate=pl.CostEstimate(flops=15000000000, bytes_accessed=10000000, transcendentals=0),
        name="pack_profiles",
    )(row_profile, col_profile, send_list.T)


def slot_address(slots, core):
    source = slots // 16
    low = turned(source // 8) * 16 + source // 128 * 4 + source % 4
    low = jnp.where(source < 512, low, LOW)
    high = (((source // 4) % 2) ^ core) * 16 + slots % 16
    return low, high


def spread_kernel(
    own_ref,
    other_ref,
    list_ref,
    row_ref,
    col_ref,
    mask_ref,
    first_top,
    first_rest,
    turn_cos,
    turn_sin,
    second_top,
    second_rest,
    out_ref,
    wide_ref,
    tall_ref,
    low_ref,
    high_ref,
    table,
    density,
):
    core = lax.axis_index("c")
    for s, ref in enumerate((own_ref, other_ref)):
        words = ref[pl.ds(s, 256, stride=3), :].T
        for part, piece in enumerate((words & 0xFFFF, words >> 16)):
            start = s * 256 + part * 128
            table[start : start + 128, :] = (piece.astype(F32) * (1.0 / SCALE)).astype(BF16)
    own_rows = own_ref[pl.ds(2, 256, stride=3), :].T
    other_rows = other_ref[pl.ds(2, 256, stride=3), :].T
    words = jnp.concatenate([own_rows[:32], other_rows[32:64]], axis=0)
    for part, piece in enumerate((words & 0xFFFF, words >> 16)):
        start = 512 + part * 64
        table[start : start + 64, :] = (piece.astype(F32) * (1.0 / SCALE)).astype(BF16)
    low, high = slot_address(list_ref[...], core)
    low_ref[...] = low
    high_ref[...] = high
    upper = lax.broadcasted_iota(I32, (8, TCAP), 0) // 4
    zero = jnp.zeros((8, TCAP), F32)

    def tile(t):
        found = dot(table[...], one_hot(low_ref[pl.ds(t, 1), :], LOW))
        place = jnp.broadcast_to(high_ref[pl.ds(t, 1), :], (8, TCAP))
        strip = [
            choose([found[h * 16 + s * 8 : h * 16 + s * 8 + 8] for h in range(32)], place)
            for s in range(2)
        ] + [zero]
        row_blocks = []
        for s in range(2):
            for part in range(2):
                for j in range(4):
                    start = 512 + part * 64 + s * 32 + j * 8
                    row_blocks.append(found[start : start + 8])
        row_sum = choose(row_blocks, place // 2)
        row_sum = jnp.where(place % 2 == upper, row_sum, pltpu.roll(row_sum, 4, 0))
        tall = jnp.where(upper == 0, row_sum, 0.0)
        row_shift = jnp.broadcast_to(row_ref[pl.ds(t, 1), :], (8, TCAP))
        for shift in (1, 2, 4):
            tall = jnp.where((row_shift & shift) != 0, pltpu.roll(tall, shift, 0), tall)
        col_shift = jnp.broadcast_to(col_ref[pl.ds(t, 1), :], (8, TCAP))
        for shift in (1, 2, 4):
            moves = (col_shift & shift) != 0
            moved = pltpu.roll(jnp.concatenate(strip, axis=0), shift, 0)
            strip = [jnp.where(moves, moved[i * 8 : i * 8 + 8], strip[i]) for i in range(3)]
        blocks = strip
        for shift in (1, 2, 4, 8):
            moves = (col_shift & (8 * shift)) != 0
            held = blocks
            blocks = []
            for i in range(min(16, len(held) + shift)):
                stay = held[i] if i < len(held) else zero
                come = held[i - shift] if i >= shift else zero
                blocks.append(jnp.where(moves, come, stay))
        return tall, jnp.concatenate(blocks, axis=0).astype(BF16)

    def step(group, carry):
        made = [tile(group * SPREAD_GROUP + i) for i in range(SPREAD_GROUP)]
        for i, (tall, wide) in enumerate(made):
            t = group * SPREAD_GROUP + i
            wide_ref[pl.ds(pl.multiple_of(t * 128, 128), 128), :] = wide
            tall_ref[pl.ds(pl.multiple_of(t * 8, 8), 8), :] = tall
            covered = mask_ref[:, pl.ds(pl.multiple_of(t * 128, 128), 128)].astype(F32)
            density[pl.ds(pl.multiple_of(t * 8, 8), 8), :] = (
                dot_last(tall.astype(BF16), wide) + MACRO_LEVEL * covered
            )
        return carry

    lax.fori_loop(0, NT // SPREAD_GROUP, step, 0)
    mixed = dot3(halves(density[...].T), (first_top[...], first_rest[...]))
    real, imag = mixed[:, :512], mixed[:, 512:]
    cos, sin = turn_cos[...], turn_sin[...]
    stacked = jnp.concatenate([real * cos + imag * sin, imag * cos - real * sin], axis=0)
    result = dot3((second_top[...], second_rest[...]), halves(stacked))
    for q in range(4):
        out_ref[q * 64 : q * 64 + 64, :] = result[:, q * 128 : q * 128 + 128]


def spread(own, other, tile_list, row_offset, col_offset, macro_mask):
    first, cos, sin, second = tables_x()
    loaded = (tile_list, row_offset, col_offset, macro_mask, *first, cos, sin, *second)
    return pl.pallas_call(
        spread_kernel,
        out_shape=(
            jax.ShapeDtypeStruct((256, 128), F32),
            jax.ShapeDtypeStruct((NT * TW, TCAP), BF16),
            jax.ShapeDtypeStruct((NT * TH, TCAP), F32),
            jax.ShapeDtypeStruct((NT, TCAP), I32),
            jax.ShapeDtypeStruct((NT, TCAP), I32),
        ),
        scratch_shapes=[pltpu.VMEM((640, 256), BF16), pltpu.VMEM((NT * TH, TW), F32)],
        compiler_params=pltpu.CompilerParams(vmem_limit_bytes=40 << 20),
        cost_estimate=pl.CostEstimate(flops=60000000000, bytes_accessed=30000000, transcendentals=0),
        name="spread",
    )(own, other, *loaded)


def column_kernel(
    got_ref, first_top, first_rest, turn_cos, turn_sin, second_top, second_rest, out_ref
):
    core = lax.axis_index("c")
    first = (first_top[...], first_rest[...])
    parts = []
    for h in range(4):
        mixed = dot3(first, halves(got_ref[pl.ds(h, 64, stride=4), :]))
        real, imag = mixed[:128], mixed[128:]
        cos, sin = turn_cos[core * 4 + h], turn_sin[core * 4 + h]
        parts += [real * cos + imag * sin, imag * cos - real * sin]
    partial = dot3(halves(jnp.concatenate(parts, axis=1)), (second_top[...], second_rest[...]))
    odd = (lax.broadcasted_iota(I32, (128, 512), 1) // 16) % 2
    out_ref[...] = jnp.where(odd * core == 1, -partial, partial)


def transform_columns(got):
    first, cos, sin, second = tables_y()
    return pl.pallas_call(
        column_kernel,
        out_shape=jax.ShapeDtypeStruct((128, 512), F32),
        compiler_params=pltpu.CompilerParams(vmem_limit_bytes=32 << 20),
        cost_estimate=pl.CostEstimate(
            flops=20000000000, bytes_accessed=20000000, transcendentals=0
        ),
        name="transform_columns",
    )(got, *first, cos, sin, *second)


def solve_kernel(
    own_ref,
    other_ref,
    back_top,
    back_rest,
    turn_cos,
    turn_sin,
    wave_top,
    wave_rest,
    out_ref,
):
    core = lax.axis_index("c")
    place = 0
    for name, size in zip(CHIPS, (2, 2, 2, 2, 4, 4)):
        place = place * size + lax.axis_index(name)
    lane = lax.broadcasted_iota(I32, (128, 512), 1)
    wave_u = lax.broadcasted_iota(I32, (128, 512), 0) + 128 * (lane // 16)
    wave_v = (place // 64) * 16 + lane % 16 + 64 * (place % 64)
    freq_u = wave_u.astype(F32) * (math.pi / GRID)
    freq_v = wave_v.astype(F32) * (math.pi / GRID)
    radius = freq_u * freq_u + freq_v * freq_v
    weight_u = jnp.where(wave_u == 0, 1.0 / GRID, 2.0 / GRID)
    weight_v = jnp.where(wave_v == 0, 1.0 / GRID, 2.0 / GRID)
    kernel = jnp.where(
        radius > 0, weight_u * weight_v / jnp.where(radius > 0, radius, 1.0), 0.0
    )
    kernel = jnp.where((lane // 16) % 2 * core == 1, -kernel, kernel)
    scaled = (own_ref[...] + other_ref[...]) * kernel
    both = jnp.concatenate([scaled * freq_v, scaled * freq_u], axis=0)
    waves = dot3(halves(both), (wave_top[...], wave_rest[...]))
    back = (back_top[...], back_rest[...])
    for h in range(4):
        cos, sin = turn_cos[core * 4 + h], turn_sin[core * 4 + h]
        maps = []
        for m in range(2):
            rows = slice(m * 128, m * 128 + 128)
            real = waves[rows, h * 256 : h * 256 + 128]
            imag = waves[rows, h * 256 + 128 : h * 256 + 256]
            out_real = real * cos - imag * sin
            out_imag = real * sin + imag * cos
            pair = [out_real, out_imag] if m == 0 else [out_imag, -out_real]
            maps.append(jnp.concatenate(pair, axis=0))
        codes = encode(dot3(back, halves(jnp.concatenate(maps, axis=1))))
        out_ref[pl.ds(h, 64, stride=4), :] = codes[:, :128] + (codes[:, 128:] << 16)


def solve_columns(own, other):
    first, cos, sin, second = tables_y()
    back = tuple(np.ascontiguousarray(part.T) for part in first)
    wave = tuple(np.ascontiguousarray(part.T) for part in second)
    return pl.pallas_call(
        solve_kernel,
        out_shape=jax.ShapeDtypeStruct((256, 128), I32),
        compiler_params=pltpu.CompilerParams(vmem_limit_bytes=32 << 20),
        cost_estimate=pl.CostEstimate(
            flops=20000000000, bytes_accessed=20000000, transcendentals=0
        ),
        name="solve_columns",
    )(own, other, *back, cos, sin, *wave)


def force_kernel(
    got_ref,
    wide_ref,
    tall_ref,
    low_ref,
    high_ref,
    wave_top,
    wave_rest,
    turn_cos,
    turn_sin,
    last_top,
    last_rest,
    fields_ref,
    out_ref,
    field,
    total,
):
    codes = got_ref[...]
    maps = [decode(codes), decode(codes >> 16)]
    columns = [maps[m][q * 64 : q * 64 + 64] for m in range(2) for q in range(4)]
    waves = dot3((wave_top[...], wave_rest[...]), halves(jnp.concatenate(columns, axis=1)))
    cos, sin = turn_cos[...], turn_sin[...]
    maps = []
    for m in range(2):
        real = waves[:128, m * 512 : m * 512 + 512]
        imag = waves[128:, m * 512 : m * 512 + 512]
        out_real = real * cos - imag * sin
        out_imag = real * sin + imag * cos
        pair = [out_imag, -out_real] if m == 0 else [out_real, out_imag]
        maps.append(jnp.concatenate(pair, axis=1))
    result = dot3(halves(jnp.concatenate(maps, axis=0)), (last_top[...], last_rest[...]))
    field[...] = result.T
    total[...] = jnp.zeros_like(total)
    lines = lax.broadcasted_iota(I32, (32, TCAP), 0)

    def weights(t):
        here = pl.ds(pl.multiple_of(t * 8, 8), 8)
        tile = field[here, :]
        pair = jnp.concatenate([tile[:, :128], tile[:, 128:]], axis=0).astype(BF16)
        crossed = dot(pair, wide_ref[pl.ds(pl.multiple_of(t * 128, 128), 128), :])
        tall = tall_ref[here, :]
        chosen = lines == high_ref[pl.ds(t, 1), :]
        tops, rests = [], []
        for m in range(2):
            force = jnp.sum(crossed[m * 8 : m * 8 + 8] * tall, axis=0, keepdims=True) * (
                1.0 / (BH * BW)
            )
            top = force.astype(BF16).astype(F32)
            tops.append(jnp.where(chosen, top, 0.0))
            rests.append(jnp.where(chosen, force - top, 0.0))
        left = jnp.concatenate(tops + rests, axis=0).astype(BF16)
        return pair, left, one_hot(low_ref[pl.ds(t, 1), :], LOW)

    def step(group, carry):
        tiles = [group * FORCE_GROUP + i for i in range(FORCE_GROUP)]
        made = [weights(t) for t in tiles]
        for t, (pair, _, _) in zip(tiles, made):
            for m in range(2):
                fields_ref[m, :, pl.ds(pl.multiple_of(t * 128, 128), 128)] = pair[
                    m * 8 : m * 8 + 8
                ]
        left = jnp.concatenate([part[1] for part in made], axis=1)
        right = jnp.concatenate([part[2] for part in made], axis=1)
        total[...] += dot_last(right, left)
        return carry

    lax.fori_loop(0, NT // FORCE_GROUP, step, 0)
    out_ref[...] = total[...] + pltpu.roll(total[...], 64, 1)


def tile_forces(got, wide, tall, low, high):
    last, cos, sin, wave = tables_x()
    last = tuple(np.ascontiguousarray(part.T) for part in last)
    wave = tuple(np.ascontiguousarray(part.T) for part in wave)
    return pl.pallas_call(
        force_kernel,
        out_shape=(
            jax.ShapeDtypeStruct((2, TH, GRID), BF16),
            jax.ShapeDtypeStruct((256, 128), F32),
        ),
        scratch_shapes=[
            pltpu.VMEM((256, 256), F32),
            pltpu.VMEM((256, 128), F32),
        ],
        compiler_params=pltpu.CompilerParams(vmem_limit_bytes=40 << 20),
        cost_estimate=pl.CostEstimate(flops=40000000000, bytes_accessed=30000000, transcendentals=0),
        name="tile_forces",
    )(got, wide, tall, low, high, *wave, cos, sin, *last)


def gather_kernel(own_ref, other_ref, low_ref, high_ref, out_ref, own, other, total):
    own[...] = own_ref[...].T
    other[...] = other_ref[...].T
    total[...] = jnp.zeros_like(total)
    lines = lax.broadcasted_iota(I32, (16, 512), 0)

    def weights(k):
        chosen = lines == high_ref[pl.ds(k, 1), :]
        tops, rests = [], []
        for m in range(2):
            force = jnp.concatenate(
                [own[pl.ds(m * 32 + k, 1), :], other[pl.ds(m * 32 + 16 + k, 1), :]], axis=1
            )
            top = force.astype(BF16).astype(F32)
            tops.append(jnp.where(chosen, top, 0.0))
            rests.append(jnp.where(chosen, force - top, 0.0))
        left = jnp.concatenate(tops + rests, axis=0).astype(BF16)
        return left, one_hot(low_ref[pl.ds(k, 1), :], LOW)

    def step(group, carry):
        made = [weights(group * GATHER_GROUP + i) for i in range(GATHER_GROUP)]
        left = jnp.concatenate([part[0] for part in made], axis=1)
        right = jnp.concatenate([part[1] for part in made], axis=1)
        total[...] += dot_last(right, left)
        return carry

    lax.fori_loop(0, CAP // GATHER_GROUP, step, 0)
    summed = total[...].T
    summed = summed[:32] + summed[32:]
    for m in range(2):
        for h in range(16):
            out_ref[m : m + 1, h * LOW : (h + 1) * LOW] = summed[m * 16 + h : m * 16 + h + 1]


def gather_forces(own, other, low, high):
    return pl.pallas_call(
        gather_kernel,
        out_shape=jax.ShapeDtypeStruct((2, CELL_DEV), F32),
        scratch_shapes=[
            pltpu.VMEM((128, 256), F32),
            pltpu.VMEM((128, 256), F32),
            pltpu.VMEM((256, 64), F32),
        ],
        compiler_params=pltpu.CompilerParams(vmem_limit_bytes=32 << 20),
        cost_estimate=pl.CostEstimate(flops=20000000000, bytes_accessed=5000000, transcendentals=0),
        name="gather_forces",
    )(own, other, low, high)


def between_chips(words):
    rows = words.shape[0]
    sent = words.reshape(256, 1, rows // 256 * 128)
    got = lax.all_to_all(sent, CHIPS, split_axis=0, concat_axis=0, tiled=True)
    return got.reshape(rows, 128)


def with_other(own):
    return own, lax.ppermute(own, "c", [(0, 1), (1, 0)])


def per_device(row_profile, col_profile, send_list, tile_list, row_offset, col_offset, macro_mask):
    words, cell_low, cell_high = pack_profiles(row_profile, col_profile, send_list)
    own, other = with_other(between_chips(words))
    lines, wide, tall, slot_low, slot_high = spread(
        own, other, tile_list, row_offset, col_offset, macro_mask
    )
    partial = transform_columns(between_chips(lines))
    maps = solve_columns(*with_other(partial))
    fields, forces = tile_forces(between_chips(maps), wide, tall, slot_low, slot_high)
    cell_force = gather_forces(*with_other(between_chips(forces)), cell_low, cell_high)
    return (fields, cell_force)


def solution(mesh):
    fine = Mesh(mesh.devices.reshape(4, 2, 2, 2, 2, 2, 4), AXES)
    placed = (P(None, AXES), P(None, AXES)) + (P(AXES, None),) * 5
    return jax.shard_map(
        per_device,
        mesh=fine,
        in_specs=placed,
        out_specs=(P(None, AXES, None), P(None, AXES)),
        check_vma=False,
    )
```

```python
import functools
import math

import jax
import jax.numpy as jnp
import numpy as np
from jax import lax
from jax.experimental import pallas as pl
from jax.experimental.pallas import tpu as pltpu
from jax.sharding import Mesh
from jax.sharding import PartitionSpec as P

GRID = 4096
BH = 4
BW = 16
TW = 128
TH = 8
NT = 32
TCAP = 256
CAP = 16
CELL_DEV = 4096
LOW = 256
MACRO_LEVEL = 4.0
SCALE = 8192.0
OCTAVES = 25.0
STEPS = 819.0
SPREAD_GROUP = 32
FORCE_GROUP = 16
F32 = jnp.float32
BF16 = jnp.bfloat16
I32 = jnp.int32

AXES = ("x", "z3", "z2", "z1", "z0", "c", "y")
CHIPS = ("z0", "z1", "z2", "z3", "x", "y")


def turned(z):
    return (z & 1) * 8 + (z & 2) * 2 + (z & 4) // 2 + (z & 8) // 8


def split_host(values):
    top = values.astype(jnp.bfloat16)
    rest = (values - top.astype(np.float64)).astype(jnp.bfloat16)
    return top, rest


@functools.cache
def tables_x():
    q = np.arange(512) // 128
    r = (np.arange(512) % 128) // 16
    f = 16 * q + np.arange(512) % 16
    t = np.arange(256) // 8
    r_in = np.arange(256) % 8
    same = r_in[:, None] == r[None, :]
    turn = np.pi * ((t[:, None] * f[None, :]) % 64) / 32.0
    first = np.concatenate([np.cos(turn) * same, -np.sin(turn) * same], axis=1)
    b = np.arange(128)
    angle = np.pi * (f[None, :] * (2 * b[:, None] + 1)) / 8192.0
    w = np.arange(64)
    wave = np.pi * ((w[:, None] * (2 * b[None, :] + 1)) % 256) / 128.0
    second = np.concatenate([np.cos(wave), np.sin(wave)], axis=1)
    return (
        split_host(first),
        np.cos(angle).astype(np.float32),
        np.sin(angle).astype(np.float32),
        split_host(second),
    )


@functools.cache
def tables_y():
    lane = np.arange(128)
    r, g = lane // 16, lane % 16
    f = np.arange(128)
    a = np.arange(64)
    a = a % 4 * 16 + turned(a // 4)
    turn = np.pi * ((f[:, None] * a[None, :]) % 128) / 64.0
    first = np.concatenate([np.cos(turn), -np.sin(turn)], axis=0)
    b = 8 * np.arange(8)[:, None] + r[None, :]
    angle = np.pi * (f[None, :, None] * (2 * b[:, None, :] + 1)) / 8192.0
    w = np.arange(512) // 16
    wave = np.pi * (((2 * b[:4, :, None] + 1) * w[None, None, :]) % 128) / 64.0
    same = g[:, None] == (np.arange(512) % 16)[None, :]
    second = np.stack([np.cos(wave) * same[None], np.sin(wave) * same[None]], axis=1)
    return (
        split_host(first),
        np.cos(angle).astype(np.float32),
        np.sin(angle).astype(np.float32),
        split_host(second.reshape(1024, 512)),
    )


def halves(values):
    top = values.astype(BF16)
    return top, (values - top.astype(F32)).astype(BF16)


def dot(left, right):
    return jnp.dot(left, right, preferred_element_type=F32)


def dot_last(left, right):
    return lax.dot_general(left, right, (((1,), (1,)), ((), ())), preferred_element_type=F32)


def dot3(left, right):
    left_top, left_rest = left
    right_top, right_rest = right
    return dot(left_top, right_top) + (dot(left_rest, right_top) + dot(left_top, right_rest))


def one_hot(index_row, extent):
    shape = (extent, index_row.shape[1])
    lines = lax.broadcasted_iota(I32, shape, 0).astype(BF16)
    index = jnp.broadcast_to(index_row.astype(BF16), shape)
    return jnp.where(lines == index, jnp.ones(shape, BF16), jnp.zeros(shape, BF16))


def choose(blocks, index):
    bit = 1
    while len(blocks) > 1:
        odd = (index & bit) != 0
        blocks = [
            jnp.where(odd, blocks[2 * i + 1], blocks[2 * i]) for i in range(len(blocks) // 2)
        ]
        bit *= 2
    return blocks[0]


def load_all(pairs, sems):
    copies = [
        pltpu.make_async_copy(source, target, sems.at[i])
        for i, (source, target) in enumerate(pairs)
    ]
    for copy in copies:
        copy.start()
    return copies


def encode(values):
    size = jnp.abs(values)
    level = (jnp.log(jnp.maximum(size, 2.0**-30)) * (1.0 / math.log(2.0)) + OCTAVES) * STEPS
    level = jnp.clip(jnp.floor(level + 0.5), 0.0, 32767.0).astype(I32)
    return level + jnp.where(values < 0, 32768, 0)


def decode(codes):
    level = codes & 0x7FFF
    size = jnp.exp((level.astype(F32) * (1.0 / STEPS) - OCTAVES) * math.log(2.0))
    size = jnp.where(level == 0, 0.0, size)
    return jnp.where((codes & 0x8000) != 0, -size, size)


def pack_kernel(
    row_hbm,
    col_hbm,
    list_hbm,
    out_ref,
    low_ref,
    high_ref,
    row_ref,
    col_ref,
    list_ref,
    table,
    cols,
    rows,
    sems,
):
    core = lax.axis_index("c")
    copies = load_all([(list_hbm, list_ref), (col_hbm, col_ref), (row_hbm, row_ref)], sems)
    target = lax.broadcasted_iota(I32, (1, 512), 1)
    chip = target // 4 % 4 * 16 + turned(target // 16 % 16)
    source = chip * 8 + ((target // 256) ^ core) * 4 + target % 4
    lines = lax.broadcasted_iota(I32, (512, 512), 0)
    move = jnp.where(lines == source, 1.0, 0.0).astype(BF16)
    copies[0].wait()
    listed = list_ref[...].astype(F32)
    empty = listed >= CELL_DEV
    high = jnp.floor(listed * (1.0 / LOW))
    low = jnp.where(empty, float(LOW), listed - high * LOW)
    high_ref[...] = dot(high.astype(BF16), move).astype(I32)
    low_ref[...] = dot(low.astype(BF16), move).astype(I32)
    for copy in copies[1:]:
        copy.wait()
    for h in range(16):
        table[h * 16 : h * 16 + 16, :] = col_ref[:, h * LOW : (h + 1) * LOW]
    table[256:320, :] = jnp.concatenate(
        [row_ref[:, h * LOW : (h + 1) * LOW].astype(F32) for h in range(16)], axis=0
    ).astype(BF16)
    upper = lax.broadcasted_iota(I32, (8, 512), 0) // 4

    def pick(k):
        found = dot(table[...], one_hot(low_ref[pl.ds(k, 1), :], LOW))
        place = jnp.broadcast_to(high_ref[pl.ds(k, 1), :], (8, 512))
        col_sum = jnp.concatenate(
            [
                choose([found[h * 16 + s * 8 : h * 16 + s * 8 + 8] for h in range(16)], place)
                for s in range(2)
            ],
            axis=0,
        )
        row_sum = choose([found[256 + h * 8 : 264 + h * 8] for h in range(8)], place // 2)
        row_sum = jnp.where(place % 2 == upper, row_sum, pltpu.roll(row_sum, 4, 0))
        return (col_sum * SCALE).astype(I32), (row_sum * SCALE).astype(I32)

    def step(j, carry):
        row_words = []
        for s in range(2):
            k = 2 * j + s
            col_a, row_a = pick(k)
            col_b, row_b = pick(k + 8)
            cols[pl.ds(pl.multiple_of(k * 16, 16), 16), :] = col_a + (col_b << 16)
            row_words.append(row_a + (row_b << 16))
        rows[pl.ds(pl.multiple_of(j * 8, 8), 8), :] = jnp.where(
            upper == 0, row_words[0], pltpu.roll(row_words[1], 4, 0)
        )
        return carry

    lax.fori_loop(0, 4, step, 0, unroll=True)
    for c in range(2):
        out_ref[pl.ds(c, 256, stride=3), :] = cols[:, c * 256 : (c + 1) * 256].T
    both = [rows[:, :256], rows[:, 256:]]
    out_ref[pl.ds(2, 256, stride=3), :] = jnp.concatenate(both + both, axis=0).T


HBM = pl.BlockSpec(memory_space=pltpu.HBM)
VMEM = pl.BlockSpec(memory_space=pltpu.VMEM)


def pack_profiles(row_profile, col_profile, send_list):
    return pl.pallas_call(
        pack_kernel,
        out_shape=(
            jax.ShapeDtypeStruct((768, 128), I32),
            jax.ShapeDtypeStruct((16, 512), I32),
            jax.ShapeDtypeStruct((16, 512), I32),
        ),
        in_specs=[HBM, HBM, HBM],
        scratch_shapes=[
            pltpu.VMEM((BH, CELL_DEV), BF16),
            pltpu.VMEM((BW, CELL_DEV), BF16),
            pltpu.VMEM((CAP, 512), I32),
            pltpu.VMEM((320, 256), BF16),
            pltpu.VMEM((128, 512), I32),
            pltpu.VMEM((32, 512), I32),
            pltpu.SemaphoreType.DMA((3,)),
        ],
        compiler_params=pltpu.CompilerParams(vmem_limit_bytes=60 << 20),
        cost_estimate=pl.CostEstimate(flops=15000000000, bytes_accessed=10000000, transcendentals=0),
        name="pack_profiles",
    )(row_profile, col_profile, send_list.T)


def slot_address(slots, core):
    source = slots // 16
    low = turned(source // 8) * 16 + source // 128 * 4 + source % 4
    low = jnp.where(source < 512, low, LOW)
    high = (((source // 4) % 2) ^ core) * 16 + slots % 16
    return low, high


def unpack(words):
    return [
        (piece.astype(F32) * (1.0 / SCALE)).astype(BF16) for piece in (words & 0xFFFF, words >> 16)
    ]


def unpack_side(side, ref):
    cols = unpack(ref[pl.ds(side, 256, stride=3), :].T)
    rows = ref[pl.ds(2, 256, stride=3), :].T
    return cols, unpack(rows[side * 32 : side * 32 + 32])


def own_half_kernel(own_ref, list_ref, table_ref, low_ref, high_ref):
    low, high = slot_address(list_ref[...], lax.axis_index("c"))
    low_ref[...] = low
    high_ref[...] = high
    cols, rows = unpack_side(0, own_ref)
    for part in range(2):
        table_ref[part * 128 : part * 128 + 128, :] = cols[part]
        table_ref[256 + part * 32 : 288 + part * 32, :] = rows[part]


def own_half(own, tile_list):
    return pl.pallas_call(
        own_half_kernel,
        out_shape=(
            jax.ShapeDtypeStruct((320, 256), BF16),
            jax.ShapeDtypeStruct((NT, TCAP), I32),
            jax.ShapeDtypeStruct((NT, TCAP), I32),
        ),
        compiler_params=pltpu.CompilerParams(vmem_limit_bytes=32 << 20),
        cost_estimate=pl.CostEstimate(
            flops=5000000000, bytes_accessed=2500000, transcendentals=0
        ),
        name="own_half",
    )(own, tile_list)


def spread_kernel(
    half_ref,
    other_ref,
    low_ref,
    high_ref,
    row_ref,
    col_ref,
    mask_ref,
    first_top,
    first_rest,
    turn_cos,
    turn_sin,
    second_top,
    second_rest,
    out_ref,
    wide_ref,
    tall_ref,
    table,
    density,
):
    cols, rows = unpack_side(1, other_ref)
    table[0:256, :] = half_ref[0:256, :]
    for part in range(2):
        start = 512 + part * 64
        table[256 + part * 128 : 384 + part * 128, :] = cols[part]
        table[start : start + 32, :] = half_ref[256 + part * 32 : 288 + part * 32, :]
        table[start + 32 : start + 64, :] = rows[part]
    upper = lax.broadcasted_iota(I32, (8, TCAP), 0) // 4
    zero = jnp.zeros((8, TCAP), F32)

    def tile(t):
        found = dot(table[...], one_hot(low_ref[pl.ds(t, 1), :], LOW))
        place = jnp.broadcast_to(high_ref[pl.ds(t, 1), :], (8, TCAP))
        strip = [
            choose([found[h * 16 + s * 8 : h * 16 + s * 8 + 8] for h in range(32)], place)
            for s in range(2)
        ] + [zero]
        row_blocks = []
        for s in range(2):
            for part in range(2):
                for j in range(4):
                    start = 512 + part * 64 + s * 32 + j * 8
                    row_blocks.append(found[start : start + 8])
        row_sum = choose(row_blocks, place // 2)
        row_sum = jnp.where(place % 2 == upper, row_sum, pltpu.roll(row_sum, 4, 0))
        tall = jnp.where(upper == 0, row_sum, 0.0)
        row_shift = jnp.broadcast_to(row_ref[pl.ds(t, 1), :], (8, TCAP))
        for shift in (1, 2, 4):
            tall = jnp.where((row_shift & shift) != 0, pltpu.roll(tall, shift, 0), tall)
        col_shift = jnp.broadcast_to(col_ref[pl.ds(t, 1), :], (8, TCAP))
        for shift in (1, 2, 4):
            moves = (col_shift & shift) != 0
            moved = pltpu.roll(jnp.concatenate(strip, axis=0), shift, 0)
            strip = [jnp.where(moves, moved[i * 8 : i * 8 + 8], strip[i]) for i in range(3)]
        blocks = strip
        for shift in (1, 2, 4, 8):
            moves = (col_shift & (8 * shift)) != 0
            held = blocks
            blocks = []
            for i in range(min(16, len(held) + shift)):
                stay = held[i] if i < len(held) else zero
                come = held[i - shift] if i >= shift else zero
                blocks.append(jnp.where(moves, come, stay))
        return tall, jnp.concatenate(blocks, axis=0).astype(BF16)

    def step(group, carry):
        made = [tile(group * SPREAD_GROUP + i) for i in range(SPREAD_GROUP)]
        for i, (tall, wide) in enumerate(made):
            t = group * SPREAD_GROUP + i
            wide_ref[pl.ds(pl.multiple_of(t * 128, 128), 128), :] = wide
            tall_ref[pl.ds(pl.multiple_of(t * 8, 8), 8), :] = tall
            covered = mask_ref[:, pl.ds(pl.multiple_of(t * 128, 128), 128)].astype(F32)
            density[pl.ds(pl.multiple_of(t * 8, 8), 8), :] = (
                dot_last(tall.astype(BF16), wide) + MACRO_LEVEL * covered
            )
        return carry

    lax.fori_loop(0, NT // SPREAD_GROUP, step, 0)
    mixed = dot3(halves(density[...].T), (first_top[...], first_rest[...]))
    real, imag = mixed[:, :512], mixed[:, 512:]
    cos, sin = turn_cos[...], turn_sin[...]
    stacked = jnp.concatenate([real * cos + imag * sin, imag * cos - real * sin], axis=0)
    result = dot3((second_top[...], second_rest[...]), halves(stacked))
    for q in range(4):
        out_ref[q * 64 : q * 64 + 64, :] = result[:, q * 128 : q * 128 + 128]


def spread(half, other, low, high, row_offset, col_offset, macro_mask):
    first, cos, sin, second = tables_x()
    loaded = (row_offset, col_offset, macro_mask, *first, cos, sin, *second)
    return pl.pallas_call(
        spread_kernel,
        out_shape=(
            jax.ShapeDtypeStruct((256, 128), F32),
            jax.ShapeDtypeStruct((NT * TW, TCAP), BF16),
            jax.ShapeDtypeStruct((NT * TH, TCAP), F32),
        ),
        scratch_shapes=[pltpu.VMEM((640, 256), BF16), pltpu.VMEM((NT * TH, TW), F32)],
        compiler_params=pltpu.CompilerParams(vmem_limit_bytes=40 << 20),
        cost_estimate=pl.CostEstimate(flops=60000000000, bytes_accessed=30000000, transcendentals=0),
        name="spread",
    )(half, other, low, high, *loaded)


def column_kernel(
    got_ref, first_top, first_rest, turn_cos, turn_sin, second_top, second_rest, out_ref
):
    core = lax.axis_index("c")
    first = (first_top[...], first_rest[...])
    parts = []
    for h in range(4):
        mixed = dot3(first, halves(got_ref[pl.ds(h, 64, stride=4), :]))
        real, imag = mixed[:128], mixed[128:]
        cos, sin = turn_cos[core * 4 + h], turn_sin[core * 4 + h]
        parts += [real * cos + imag * sin, imag * cos - real * sin]
    partial = dot3(halves(jnp.concatenate(parts, axis=1)), (second_top[...], second_rest[...]))
    odd = (lax.broadcasted_iota(I32, (128, 512), 1) // 16) % 2
    out_ref[...] = jnp.where(odd * core == 1, -partial, partial)


def transform_columns(got):
    first, cos, sin, second = tables_y()
    return pl.pallas_call(
        column_kernel,
        out_shape=jax.ShapeDtypeStruct((128, 512), F32),
        compiler_params=pltpu.CompilerParams(vmem_limit_bytes=32 << 20),
        cost_estimate=pl.CostEstimate(
            flops=20000000000, bytes_accessed=20000000, transcendentals=0
        ),
        name="transform_columns",
    )(got, *first, cos, sin, *second)


def solve_kernel(
    own_ref,
    other_ref,
    back_top,
    back_rest,
    turn_cos,
    turn_sin,
    wave_top,
    wave_rest,
    out_ref,
):
    core = lax.axis_index("c")
    place = 0
    for name, size in zip(CHIPS, (2, 2, 2, 2, 4, 4)):
        place = place * size + lax.axis_index(name)
    lane = lax.broadcasted_iota(I32, (128, 512), 1)
    wave_u = lax.broadcasted_iota(I32, (128, 512), 0) + 128 * (lane // 16)
    wave_v = (place // 64) * 16 + lane % 16 + 64 * (place % 64)
    freq_u = wave_u.astype(F32) * (math.pi / GRID)
    freq_v = wave_v.astype(F32) * (math.pi / GRID)
    radius = freq_u * freq_u + freq_v * freq_v
    weight_u = jnp.where(wave_u == 0, 1.0 / GRID, 2.0 / GRID)
    weight_v = jnp.where(wave_v == 0, 1.0 / GRID, 2.0 / GRID)
    kernel = jnp.where(
        radius > 0, weight_u * weight_v / jnp.where(radius > 0, radius, 1.0), 0.0
    )
    kernel = jnp.where((lane // 16) % 2 * core == 1, -kernel, kernel)
    scaled = (own_ref[...] + other_ref[...]) * kernel
    both = jnp.concatenate([scaled * freq_v, scaled * freq_u], axis=0)
    waves = dot3(halves(both), (wave_top[...], wave_rest[...]))
    back = (back_top[...], back_rest[...])
    for h in range(4):
        cos, sin = turn_cos[core * 4 + h], turn_sin[core * 4 + h]
        maps = []
        for m in range(2):
            rows = slice(m * 128, m * 128 + 128)
            real = waves[rows, h * 256 : h * 256 + 128]
            imag = waves[rows, h * 256 + 128 : h * 256 + 256]
            out_real = real * cos - imag * sin
            out_imag = real * sin + imag * cos
            pair = [out_real, out_imag] if m == 0 else [out_imag, -out_real]
            maps.append(jnp.concatenate(pair, axis=0))
        codes = encode(dot3(back, halves(jnp.concatenate(maps, axis=1))))
        out_ref[pl.ds(h, 64, stride=4), :] = codes[:, :128] + (codes[:, 128:] << 16)


def solve_columns(own, other):
    first, cos, sin, second = tables_y()
    back = tuple(np.ascontiguousarray(part.T) for part in first)
    wave = tuple(np.ascontiguousarray(part.T) for part in second)
    return pl.pallas_call(
        solve_kernel,
        out_shape=jax.ShapeDtypeStruct((256, 128), I32),
        compiler_params=pltpu.CompilerParams(vmem_limit_bytes=32 << 20),
        cost_estimate=pl.CostEstimate(
            flops=20000000000, bytes_accessed=20000000, transcendentals=0
        ),
        name="solve_columns",
    )(own, other, *back, cos, sin, *wave)


def force_kernel(
    got_ref,
    wide_ref,
    tall_ref,
    low_ref,
    high_ref,
    wave_top,
    wave_rest,
    turn_cos,
    turn_sin,
    last_top,
    last_rest,
    fields_ref,
    out_ref,
    field,
    total,
):
    codes = got_ref[...]
    maps = [decode(codes), decode(codes >> 16)]
    columns = [maps[m][q * 64 : q * 64 + 64] for m in range(2) for q in range(4)]
    waves = dot3((wave_top[...], wave_rest[...]), halves(jnp.concatenate(columns, axis=1)))
    cos, sin = turn_cos[...], turn_sin[...]
    maps = []
    for m in range(2):
        real = waves[:128, m * 512 : m * 512 + 512]
        imag = waves[128:, m * 512 : m * 512 + 512]
        out_real = real * cos - imag * sin
        out_imag = real * sin + imag * cos
        pair = [out_imag, -out_real] if m == 0 else [out_real, out_imag]
        maps.append(jnp.concatenate(pair, axis=1))
    result = dot3(halves(jnp.concatenate(maps, axis=0)), (last_top[...], last_rest[...]))
    field[...] = result.T
    total[...] = jnp.zeros_like(total)
    lines = lax.broadcasted_iota(I32, (32, TCAP), 0)

    def weights(t):
        here = pl.ds(pl.multiple_of(t * 8, 8), 8)
        tile = field[here, :]
        pair = jnp.concatenate([tile[:, :128], tile[:, 128:]], axis=0).astype(BF16)
        crossed = dot(pair, wide_ref[pl.ds(pl.multiple_of(t * 128, 128), 128), :])
        tall = tall_ref[here, :]
        chosen = lines == high_ref[pl.ds(t, 1), :]
        tops, rests = [], []
        for m in range(2):
            force = jnp.sum(crossed[m * 8 : m * 8 + 8] * tall, axis=0, keepdims=True) * (
                1.0 / (BH * BW)
            )
            top = force.astype(BF16).astype(F32)
            tops.append(jnp.where(chosen, top, 0.0))
            rests.append(jnp.where(chosen, force - top, 0.0))
        left = jnp.concatenate(tops + rests, axis=0).astype(BF16)
        return pair, left, one_hot(low_ref[pl.ds(t, 1), :], LOW)

    def step(group, carry):
        tiles = [group * FORCE_GROUP + i for i in range(FORCE_GROUP)]
        made = [weights(t) for t in tiles]
        for t, (pair, _, _) in zip(tiles, made):
            for m in range(2):
                fields_ref[m, :, pl.ds(pl.multiple_of(t * 128, 128), 128)] = pair[
                    m * 8 : m * 8 + 8
                ]
        left = jnp.concatenate([part[1] for part in made], axis=1)
        right = jnp.concatenate([part[2] for part in made], axis=1)
        total[...] += dot_last(right, left)
        return carry

    lax.fori_loop(0, NT // FORCE_GROUP, step, 0)
    out_ref[...] = total[...] + pltpu.roll(total[...], 64, 1)


def tile_forces(got, wide, tall, low, high):
    last, cos, sin, wave = tables_x()
    last = tuple(np.ascontiguousarray(part.T) for part in last)
    wave = tuple(np.ascontiguousarray(part.T) for part in wave)
    return pl.pallas_call(
        force_kernel,
        out_shape=(
            jax.ShapeDtypeStruct((2, TH, GRID), BF16),
            jax.ShapeDtypeStruct((256, 128), F32),
        ),
        scratch_shapes=[
            pltpu.VMEM((256, 256), F32),
            pltpu.VMEM((256, 128), F32),
        ],
        compiler_params=pltpu.CompilerParams(vmem_limit_bytes=40 << 20),
        cost_estimate=pl.CostEstimate(flops=40000000000, bytes_accessed=30000000, transcendentals=0),
        name="tile_forces",
    )(got, wide, tall, low, high, *wave, cos, sin, *last)


def gather_part(side, got_ref, low_ref, high_ref, got):
    got[...] = got_ref[...].T
    lines = lax.broadcasted_iota(I32, (16, 256), 0)
    here = slice(side * 256, side * 256 + 256)
    lefts, rights = [], []
    for k in range(CAP):
        chosen = lines == high_ref[k : k + 1, here]
        tops, rests = [], []
        for m in range(2):
            row = m * 32 + side * 16 + k
            force = got[row : row + 1, :]
            top = force.astype(BF16).astype(F32)
            tops.append(jnp.where(chosen, top, 0.0))
            rests.append(jnp.where(chosen, force - top, 0.0))
        lefts.append(jnp.concatenate(tops + rests, axis=0).astype(BF16))
        rights.append(one_hot(low_ref[k : k + 1, here], LOW))
    return dot_last(jnp.concatenate(rights, axis=1), jnp.concatenate(lefts, axis=1))


def gather_own_kernel(got_ref, low_ref, high_ref, out_ref, got):
    out_ref[...] = gather_part(0, got_ref, low_ref, high_ref, got)


def gather_kernel(own_ref, got_ref, low_ref, high_ref, out_ref, got):
    summed = (own_ref[...] + gather_part(1, got_ref, low_ref, high_ref, got)).T
    summed = summed[:32] + summed[32:]
    for m in range(2):
        for h in range(16):
            out_ref[m : m + 1, h * LOW : (h + 1) * LOW] = summed[m * 16 + h : m * 16 + h + 1]


def gather_call(kernel, shape, name):
    return pl.pallas_call(
        kernel,
        out_shape=jax.ShapeDtypeStruct(shape, F32),
        scratch_shapes=[pltpu.VMEM((128, 256), F32)],
        compiler_params=pltpu.CompilerParams(vmem_limit_bytes=32 << 20),
        cost_estimate=pl.CostEstimate(
            flops=10000000000, bytes_accessed=2500000, transcendentals=0
        ),
        name=name,
    )


def gather_forces(own, other, low, high):
    part = gather_call(gather_own_kernel, (256, 64), "gather_own")(own, low, high)
    return gather_call(gather_kernel, (2, CELL_DEV), "gather_forces")(part, other, low, high)


def between_chips(words):
    rows = words.shape[0]
    sent = words.reshape(256, 1, rows // 256 * 128)
    got = lax.all_to_all(sent, CHIPS, split_axis=0, concat_axis=0, tiled=True)
    return got.reshape(rows, 128)


def with_other(own):
    return own, lax.ppermute(own, "c", [(0, 1), (1, 0)])


def per_device(row_profile, col_profile, send_list, tile_list, row_offset, col_offset, macro_mask):
    words, cell_low, cell_high = pack_profiles(row_profile, col_profile, send_list)
    own, other = with_other(between_chips(words))
    half, slot_low, slot_high = own_half(own, tile_list)
    lines, wide, tall = spread(
        half, other, slot_low, slot_high, row_offset, col_offset, macro_mask
    )
    partial = transform_columns(between_chips(lines))
    maps = solve_columns(*with_other(partial))
    fields, forces = tile_forces(between_chips(maps), wide, tall, slot_low, slot_high)
    cell_force = gather_forces(*with_other(between_chips(forces)), cell_low, cell_high)
    return (fields, cell_force)


def solution(mesh):
    fine = Mesh(mesh.devices.reshape(4, 2, 2, 2, 2, 2, 4), AXES)
    placed = (P(None, AXES), P(None, AXES)) + (P(AXES, None),) * 5
    return jax.shard_map(
        per_device,
        mesh=fine,
        in_specs=placed,
        out_specs=(P(None, AXES, None), P(None, AXES)),
        check_vma=False,
    )
```
